32 devices in a mesh: dp: 4 (over y, x), vocab: 8 (over z, core).
Axes of the slice: x: 2, y: 2, z: 4, core: 2. Of those that a mesh axis runs over, the one named last changes fastest.
Arguments:
- hidden: bfloat16 [1024, 4096], P(('dp', 'vocab')), may hold values from -48 to 48
- weight: bfloat16 [8192, 4096], P('vocab'), may hold values from -3 to 3
- teacher: bfloat16 [1024, 8192], P('dp', 'vocab'), may hold values from 0 to 0.002, as said below
- block_ids: int32 [8, 64], P('dp'), may hold values from 0 to 63, as said below
Outputs:
- grad_hidden: bfloat16 [1024, 4096], P(('dp', 'vocab'))
- grad_weight: bfloat16 [8192, 4096], P('vocab', 'dp')
The draws below stay inside these ranges and needn't reach their ends.
Inputs may be any that keep to these rules, and one draw needn't show every extreme that they name: `block_ids`: row b lists 64 different vocabulary blocks in no fixed order; frequent blocks recur over many rows. `teacher`: all entries are positive.
All inputs are finite; a program needn't handle non-finite values.
Results may differ from the reference program's by a relative error of at most 0.0051.
Values may be sent and summed in bfloat16 or wider, within the bound.
No kernel may reach another device: no remote copies, remote signals or barrier semaphores. Data moves between devices by JAX's collectives and lax.ppermute only.
A program may use at most 128 MiB of HBM per device.

```python
import math
import jax
import jax.numpy as jnp
from jax import lax

D = 4096
BLK = 128
K = 64
VB = 64
TOKENS = 1024
TB = 8


def weight_row(key, vocab_index):
    noise_row = jnp.clip(jax.random.normal(jax.random.fold_in(jax.random.fold_in(key, 31), vocab_index), (D,), jnp.float32), -6.0, 6.0)
    row_level = jnp.exp(jax.random.uniform(jax.random.fold_in(jax.random.fold_in(key, 32), vocab_index), (), jnp.float32, math.log(0.3), 0.0))
    row_level = row_level * (1.0 + 2.0 * vocab_index.astype(jnp.float32) / (VB * BLK))
    row_value = noise_row * row_level / math.sqrt(D)
    return row_value.astype(jnp.bfloat16).astype(jnp.float32)


def draw_weight(key, part):
    indices = jnp.arange(VB * BLK, dtype=jnp.int32)
    rows = jax.vmap(lambda index: weight_row(key, index))(indices)
    return rows.astype(jnp.bfloat16)


def draw_hidden(key, part):
    values = jnp.clip(jax.random.normal(jax.random.fold_in(key, 21), (TOKENS, D), jnp.float32), -6.0, 6.0)
    return values.astype(jnp.bfloat16)


def draw_teacher(key, part):
    slot_of = (jnp.arange(K * BLK, dtype=jnp.int32) // BLK).astype(jnp.float32)
    factor = 0.5 + slot_of / (K - 1)
    values = jnp.exp(jax.random.uniform(jax.random.fold_in(key, 41), (TOKENS, K * BLK), jnp.float32, math.log(1e-06), math.log(0.0008)))
    return (values * factor[None, :]).astype(jnp.bfloat16)


def draw_block_ids(key, part):
    popularity = jax.random.randint(jax.random.fold_in(key, 51), (VB,), 0, 4, jnp.int32)
    noise = jax.random.randint(jax.random.fold_in(key, 52), (TB, VB), 0, 1024, jnp.int32)
    block_range = jnp.arange(VB, dtype=jnp.int32)
    row_range = jnp.arange(TB, dtype=jnp.int32)
    forced = (row_range[:, None] == 0) & (block_range[None, :] == 0) | (row_range[:, None] == TB - 1) & (block_range[None, :] == VB - 1)
    scores = noise + 256 * popularity[None, :] + 4096 * forced.astype(jnp.int32)
    scores = scores * VB + block_range[None, :]
    top_scores, chosen = lax.top_k(scores, K)
    order_keys = jax.random.randint(jax.random.fold_in(key, 53), (TB, K), 0, 65536, jnp.int32) * K + jnp.arange(K, dtype=jnp.int32)[None, :]
    order = jnp.argsort(order_keys, axis=1, stable=True)
    return jnp.take_along_axis(chosen.astype(jnp.int32), order.astype(jnp.int32), axis=1).astype(jnp.int32)


def setup_inputs(seed: int = 0) -> dict:
    arg_keys = jax.random.split(jax.random.key(seed), 5)
    hidden = draw_hidden(jax.random.fold_in(arg_keys[4], 71), 0)
    weight = draw_weight(jax.random.fold_in(arg_keys[4], 71), 0)
    teacher = draw_teacher(jax.random.fold_in(arg_keys[4], 71), 0)
    block_ids = draw_block_ids(jax.random.fold_in(arg_keys[4], 71), 0)
    return dict(hidden=hidden, weight=weight, teacher=teacher, block_ids=block_ids)


loss_scale = 1024.0


def reference(hidden, weight, teacher, block_ids):
    logits = jnp.dot(hidden, weight.T, preferred_element_type=jnp.float32)
    row_top = jnp.max(logits, axis=1, keepdims=True)
    exp_terms = jnp.exp(logits - row_top)
    row_total = jnp.sum(exp_terms, axis=1, keepdims=True)
    teacher_tiles = teacher.astype(jnp.float32).reshape(TB, BLK, K, BLK)
    row_mass = jnp.sum(teacher_tiles, axis=(2, 3)).reshape(TOKENS, 1)
    placed = jnp.zeros((TB, VB, BLK, BLK), jnp.float32)
    rows_index = jnp.arange(TB, dtype=jnp.int32)[:, None]
    placed = placed.at[rows_index, block_ids.astype(jnp.int32)].set(jnp.transpose(teacher_tiles, (0, 2, 1, 3)))
    target = jnp.transpose(placed, (0, 2, 1, 3)).reshape(TOKENS, VB * BLK)
    grad_logits = (loss_scale * (row_mass * (exp_terms / row_total) - target)).astype(jnp.bfloat16)
    grad_hidden = jnp.dot(grad_logits, weight, preferred_element_type=jnp.float32).astype(jnp.bfloat16)
    grad_weight = jnp.dot(grad_logits.T, hidden, preferred_element_type=jnp.float32).astype(jnp.bfloat16)
    return (grad_hidden, grad_weight)
```

```python
import jax
import jax.numpy as jnp
from jax import lax
from jax.experimental import pallas as pl
from jax.experimental.pallas import tpu as pltpu
from jax.sharding import PartitionSpec as P

BLK = 128
TILE_ROWS = 16


loss_scale = 1024.0


def plain_shards(hidden, weight, teacher, block_ids):
    vocab_rows = weight.shape[0]
    owned_blocks = vocab_rows // BLK
    vocab_pos = lax.axis_index("vocab")
    full_hidden = lax.all_gather(hidden, "vocab", axis=0, tiled=True)
    token_count = full_hidden.shape[0]
    width = full_hidden.shape[1]
    logits = lax.dot_general(
        full_hidden, weight, (((1,), (1,)), ((), ())), preferred_element_type=jnp.float32
    )
    row_top = lax.pmax(jnp.max(logits, axis=1), "vocab")
    exp_terms = jnp.exp(logits - row_top[:, None])
    row_total = lax.psum(jnp.sum(exp_terms, axis=1), "vocab")
    block_count = token_count // BLK
    first_block = vocab_pos * owned_blocks
    block_range = jnp.arange(owned_blocks, dtype=jnp.int32)
    tile_cols = lax.all_gather(teacher, "vocab", axis=1, tiled=True)
    slot_count = tile_cols.shape[1] // BLK
    owned = block_ids - first_block
    onehot = (owned[:, :, None] == block_range[None, None, :]).astype(jnp.bfloat16)
    shaped = tile_cols.reshape(block_count, BLK, slot_count, BLK)
    target = jnp.einsum("bkv,btkc->btvc", onehot, shaped, preferred_element_type=jnp.float32)
    row_mass = jnp.sum(tile_cols, axis=1, dtype=jnp.float32)
    target = target.reshape(token_count, vocab_rows)
    grad_logits = (
        loss_scale * (row_mass[:, None] * (exp_terms / row_total[:, None]) - target)
    ).astype(jnp.bfloat16)
    grad_hidden = lax.psum_scatter(
        jnp.dot(grad_logits, weight, preferred_element_type=jnp.float32),
        "vocab",
        scatter_dimension=0,
        tiled=True,
    ).astype(jnp.bfloat16)
    data_count = lax.axis_size("dp")
    quarter = width // data_count
    split_hidden = full_hidden.reshape(token_count, data_count, quarter)
    quarter_rows = lax.all_to_all(
        split_hidden, "dp", split_axis=1, concat_axis=0, tiled=True
    ).reshape(token_count * data_count, quarter)
    grad_weight = lax.dot_general(
        lax.all_gather(grad_logits, "dp", axis=0, tiled=True),
        quarter_rows,
        (((0,), (0,)), ((), ())),
        preferred_element_type=jnp.float32,
    ).astype(jnp.bfloat16)
    return (grad_hidden, grad_weight)


def swap(x, axis, bits):
    return lax.ppermute(x, axis, [(i, i ^ bits) for i in range(lax.axis_size(axis))])


def take_tiles(slots, teacher, rows, chips):
    blocks, owned = slots.shape

    def body(slots_ref, teacher_ref, out_ref, sem):
        me = lax.axis_index("vocab")
        core = lax.rem(me, 2)
        chip = me // 2
        copies = []
        for h in range(2):
            for j in range(chips):
                source = ((chip ^ j) * 2 + (core ^ h)) * rows
                block = source // BLK
                for v in range(owned):
                    copies.append(
                        pltpu.make_async_copy(
                            teacher_ref.at[
                                pl.ds(pl.multiple_of(source, rows), rows),
                                pl.ds(pl.multiple_of(slots_ref[block, v] * BLK, BLK), BLK),
                            ],
                            out_ref.at[pl.ds((h * chips + j) * rows, rows), pl.ds(v * BLK, BLK)],
                            sem.at[len(copies)],
                        )
                    )
        for copy in copies:
            copy.start()
        for copy in copies:
            copy.wait()

    return pl.pallas_call(
        body,
        out_shape=jax.ShapeDtypeStruct((teacher.shape[0], owned * BLK), teacher.dtype),
        in_specs=[
            pl.BlockSpec(memory_space=pltpu.SMEM),
            pl.BlockSpec(memory_space=pl.ANY),
        ],
        out_specs=pl.BlockSpec(memory_space=pltpu.VMEM),
        scratch_shapes=[pltpu.SemaphoreType.DMA((2 * chips * owned,))],
        cost_estimate=pl.CostEstimate(flops=0, bytes_accessed=2**20, transcendentals=0),
    )(slots, teacher)


def shards(hidden, weight, teacher, block_ids):
    vocab_size = lax.axis_size("vocab")
    data_size = lax.axis_size("dp")
    rows, width = hidden.shape
    vocab_rows = weight.shape[0]
    owned_blocks = vocab_rows // BLK
    chips = vocab_size // 2
    tokens = vocab_size * rows
    half_tokens = chips * rows
    me = lax.axis_index("vocab")
    core = lax.rem(me, 2)
    chip = me // 2
    data_pos = lax.axis_index("dp")

    gathered = lax.all_gather(teacher, "vocab", axis=1, tiled=True)
    own = jnp.concatenate([hidden] + [swap(hidden, "vocab", 2 * j) for j in range(1, chips)])
    other = swap(own, "vocab", 1)

    def logits_of(part):
        return lax.dot_general(
            part, weight, (((1,), (1,)), ((), ())), preferred_element_type=jnp.float32
        )

    logits = [logits_of(own), logits_of(other)]

    quarter = width // data_size
    cols = [
        lax.dynamic_slice_in_dim(own, (data_pos ^ r) * quarter, quarter, axis=1)
        for r in range(data_size)
    ]
    cols = jnp.stack([cols[0]] + [swap(cols[r], "dp", r) for r in range(1, data_size)])
    cols = jnp.stack([cols, swap(cols, "vocab", 1)], axis=1).reshape(data_size * tokens, quarter)

    top = jnp.concatenate([jnp.max(x, axis=1) for x in logits])
    total = jnp.concatenate([
        jnp.sum(jnp.exp(x - jnp.max(x, axis=1)[:, None]), axis=1) for x in logits
    ])
    mass = jnp.sum(teacher, axis=1, dtype=jnp.float32)
    bits = 1
    while bits < vocab_size:
        got = swap(jnp.stack([top, total, mass]), "vocab", bits)
        grid = got[:2].reshape(2, 2, chips, rows)
        if bits == 1:
            grid = grid[:, ::-1]
        else:
            grid = jnp.stack([grid[:, :, j ^ (bits // 2)] for j in range(chips)], axis=2)
        got_top, got_total = grid.reshape(2, tokens)
        new_top = jnp.maximum(top, got_top)
        total = total * jnp.exp(top - new_top) + got_total * jnp.exp(got_top - new_top)
        top = new_top
        mass = mass + got[2]
        bits *= 2
    groups = [(chip ^ j) * 2 + (core ^ h) for h in range(2) for j in range(chips)]
    mass = jnp.concatenate([lax.dynamic_slice_in_dim(mass, g * rows, rows) for g in groups])

    first_block = me * owned_blocks
    wanted = first_block + jnp.arange(owned_blocks, dtype=jnp.int32)
    match = block_ids[:, None, :] == wanted[None, :, None]
    slots = jnp.argmax(match, axis=2).astype(jnp.int32)
    listed = jnp.any(match, axis=2).astype(jnp.float32) * loss_scale
    tiles = take_tiles(slots, gathered, rows, chips)
    group_block = jnp.stack(groups) * rows // BLK
    tile_scale = jnp.take(listed, group_block, axis=0)
    tile_scale = jnp.broadcast_to(
        tile_scale[:, None, :, None], (vocab_size, rows, owned_blocks, BLK)
    ).reshape(tokens, vocab_rows)

    factor = loss_scale * mass / total
    grads = []
    for h in range(2):
        part = slice(h * half_tokens, (h + 1) * half_tokens)
        grads.append(
            (
                factor[part, None] * jnp.exp(logits[h] - top[part, None])
                - tile_scale[part] * tiles[part].astype(jnp.float32)
            ).astype(jnp.bfloat16)
        )
    grad_logits = jnp.concatenate(grads)

    all_grads = jnp.concatenate(
        [grad_logits] + [swap(grad_logits, "dp", r) for r in range(1, data_size)]
    )
    grad_weight = lax.dot_general(
        all_grads, cols, (((0,), (0,)), ((), ())), preferred_element_type=jnp.float32
    ).astype(jnp.bfloat16)

    sent = swap(
        jnp.dot(grads[1], weight, preferred_element_type=jnp.float32).astype(jnp.bfloat16),
        "vocab",
        1,
    )
    share = jnp.dot(grads[0], weight, preferred_element_type=jnp.float32) + sent.astype(jnp.float32)
    result = share[:rows]
    for j in range(1, chips):
        piece = share[j * rows : (j + 1) * rows].astype(jnp.bfloat16)
        result = result + swap(piece, "vocab", 2 * j).astype(jnp.float32)
    return (result.astype(jnp.bfloat16), grad_weight)


def solution(mesh):
    placed = (P(("dp", "vocab"), None), P("vocab", None), P("dp", "vocab"), P("dp", None))

    def run(hidden, weight, teacher, block_ids):
        rows = hidden.shape[0] // (mesh.shape["dp"] * mesh.shape["vocab"])
        paired = all(size & (size - 1) == 0 for size in mesh.shape.values())
        form = shards if paired and rows % TILE_ROWS == 0 else plain_shards
        return jax.shard_map(
            form,
            mesh=mesh,
            in_specs=placed,
            out_specs=(P(("dp", "vocab"), None), P("vocab", "dp")),
            check_vma=False,
        )(hidden, weight, teacher, block_ids)

    return run
```

```python
import jax
import jax.numpy as jnp
from jax import lax
from jax.experimental import pallas as pl
from jax.experimental.pallas import tpu as pltpu
from jax.sharding import PartitionSpec as P

BLK = 128
TILE_ROWS = 16


loss_scale = 1024.0


def plain_shards(hidden, weight, teacher, block_ids):
    vocab_rows = weight.shape[0]
    owned_blocks = vocab_rows // BLK
    vocab_pos = lax.axis_index("vocab")
    full_hidden = lax.all_gather(hidden, "vocab", axis=0, tiled=True)
    token_count = full_hidden.shape[0]
    width = full_hidden.shape[1]
    logits = lax.dot_general(
        full_hidden, weight, (((1,), (1,)), ((), ())), preferred_element_type=jnp.float32
    )
    row_top = lax.pmax(jnp.max(logits, axis=1), "vocab")
    exp_terms = jnp.exp(logits - row_top[:, None])
    row_total = lax.psum(jnp.sum(exp_terms, axis=1), "vocab")
    block_count = token_count // BLK
    first_block = vocab_pos * owned_blocks
    block_range = jnp.arange(owned_blocks, dtype=jnp.int32)
    tile_cols = lax.all_gather(teacher, "vocab", axis=1, tiled=True)
    slot_count = tile_cols.shape[1] // BLK
    owned = block_ids - first_block
    onehot = (owned[:, :, None] == block_range[None, None, :]).astype(jnp.bfloat16)
    shaped = tile_cols.reshape(block_count, BLK, slot_count, BLK)
    target = jnp.einsum("bkv,btkc->btvc", onehot, shaped, preferred_element_type=jnp.float32)
    row_mass = jnp.sum(tile_cols, axis=1, dtype=jnp.float32)
    target = target.reshape(token_count, vocab_rows)
    grad_logits = (
        loss_scale * (row_mass[:, None] * (exp_terms / row_total[:, None]) - target)
    ).astype(jnp.bfloat16)
    grad_hidden = lax.psum_scatter(
        jnp.dot(grad_logits, weight, preferred_element_type=jnp.float32),
        "vocab",
        scatter_dimension=0,
        tiled=True,
    ).astype(jnp.bfloat16)
    data_count = lax.axis_size("dp")
    quarter = width // data_count
    split_hidden = full_hidden.reshape(token_count, data_count, quarter)
    quarter_rows = lax.all_to_all(
        split_hidden, "dp", split_axis=1, concat_axis=0, tiled=True
    ).reshape(token_count * data_count, quarter)
    grad_weight = lax.dot_general(
        lax.all_gather(grad_logits, "dp", axis=0, tiled=True),
        quarter_rows,
        (((0,), (0,)), ((), ())),
        preferred_element_type=jnp.float32,
    ).astype(jnp.bfloat16)
    return (grad_hidden, grad_weight)


def swap(x, axis, bits):
    return lax.ppermute(x, axis, [(i, i ^ bits) for i in range(lax.axis_size(axis))])


ANY = pl.BlockSpec(memory_space=pl.ANY)
WHOLE = pl.BlockSpec(memory_space=pltpu.VMEM)
SCALARS = pl.BlockSpec(memory_space=pltpu.SMEM)
MIB = 2**20


def in_hbm(x):
    return pltpu.with_memory_space_constraint(x, pltpu.HBM)


def place_on_mesh():
    me = lax.axis_index("vocab")
    return me // 2, lax.rem(me, 2)


def as_row(column):
    n = column.shape[0]
    same = lax.broadcasted_iota(jnp.int32, (n, n), 0) == lax.broadcasted_iota(jnp.int32, (n, n), 1)
    return jnp.sum(jnp.where(same, column, 0.0), axis=0, keepdims=True)


def as_column(row):
    n = row.shape[1]
    same = lax.broadcasted_iota(jnp.int32, (n, n), 0) == lax.broadcasted_iota(jnp.int32, (n, n), 1)
    return jnp.sum(jnp.where(same, row, 0.0), axis=1, keepdims=True)


def merge(stats):
    top = stats[0][0:1]
    for x in stats[1:]:
        top = jnp.maximum(top, x[0:1])
    total = sum(x[1:2] * jnp.exp(x[0:1] - top) for x in stats)
    mass = sum(x[2:3] for x in stats)
    return top, total, mass


def cost(flops, ops):
    return pl.CostEstimate(
        flops=flops, bytes_accessed=sum(op.size * 2 for op in ops), transcendentals=0
    )


def logits_and_stats(own, other, rows, weight, mass, quarter, parts=4):
    half, width = own.shape
    chips = half // rows
    tokens = 2 * half
    vocab_rows = weight.shape[0]
    step = vocab_rows // parts
    groups = width // quarter

    def body(*refs):
        piece_refs, refs = refs[:2], refs[2:]
        weight_ref, mass_ref, out_ref, stats_ref, refs = *refs[:4], refs[4:]
        cols_refs, refs = refs[:groups], refs[groups:]
        held, held_weight, sems, piece_sems, cols_sems = refs
        chip, core = place_on_mesh()
        data_pos = lax.axis_index("dp")
        loads = []
        for h in range(2):
            for j in range(chips):
                start = ((chip ^ j) * 2 + (core ^ h)) * rows
                n = h * chips + j
                loads.append(
                    pltpu.make_async_copy(
                        piece_refs[h].at[pl.ds(j * rows, rows)],
                        held.at[pl.ds(pl.multiple_of(start, rows), rows)],
                        piece_sems.at[n],
                    )
                )
                loads[n].start()
        copies = []
        for k in range(parts):
            some = pl.ds(k * step, step)
            copies.append(
                pltpu.make_async_copy(weight_ref.at[some], held_weight.at[some], sems.at[k])
            )
            copies[k].start()
        for load in loads:
            load.wait()
        stores = []
        for r in range(groups):
            column = pl.multiple_of((data_pos ^ r) * quarter, quarter)
            for j in range(chips):
                start = ((chip ^ j) * 2 + core) * rows
                stores.append(
                    pltpu.make_async_copy(
                        held.at[pl.ds(pl.multiple_of(start, rows), rows), pl.ds(column, quarter)],
                        cols_refs[r].at[pl.ds(j * rows, rows)],
                        cols_sems.at[r, j],
                    )
                )
                stores[-1].start()
        for k in range(parts):
            copies[k].wait()
            out_ref[:, k * step : (k + 1) * step] = lax.dot_general(
                held[...],
                held_weight[k * step : (k + 1) * step],
                (((1,), (1,)), ((), ())),
                preferred_element_type=jnp.float32,
            )
        top = jnp.max(out_ref[...], axis=1, keepdims=True)
        total = jnp.sum(jnp.exp(out_ref[...] - top), axis=1, keepdims=True)
        stats_ref[0:1] = as_row(top)
        stats_ref[1:2] = as_row(total)
        stats_ref[2:3] = mass_ref[...]
        stats_ref[3:8] = jnp.zeros((5, tokens), jnp.float32)
        for store in stores:
            store.wait()

    ops = [own, other, in_hbm(weight), mass]
    return pl.pallas_call(
        body,
        out_shape=[
            jax.ShapeDtypeStruct((tokens, vocab_rows), jnp.float32),
            jax.ShapeDtypeStruct((8, tokens), jnp.float32),
        ]
        + [jax.ShapeDtypeStruct((half, quarter), weight.dtype)] * groups,
        in_specs=[ANY] * 3 + [WHOLE],
        out_specs=[WHOLE, WHOLE] + [ANY] * groups,
        scratch_shapes=[
            pltpu.VMEM((tokens, width), weight.dtype),
            pltpu.VMEM(weight.shape, weight.dtype),
            pltpu.SemaphoreType.DMA((parts,)),
            pltpu.SemaphoreType.DMA((2 * chips,)),
            pltpu.SemaphoreType.DMA((groups, chips)),
        ],
        compiler_params=pltpu.CompilerParams(vmem_limit_bytes=32 * MIB),
        cost_estimate=cost(2 * tokens * weight.size, ops),
    )(*ops)


def merge_pair(a, b):
    def body(a_ref, b_ref, out_ref):
        for k, row in enumerate(merge([a_ref[...], b_ref[...]])):
            out_ref[k : k + 1] = row
        out_ref[3:8] = jnp.zeros((5, a.shape[1]), jnp.float32)

    return pl.pallas_call(
        body,
        out_shape=jax.ShapeDtypeStruct(a.shape, a.dtype),
        in_specs=[WHOLE, WHOLE],
        out_specs=WHOLE,
        compiler_params=pltpu.CompilerParams(vmem_limit_bytes=MIB),
        cost_estimate=cost(0, (a, b)),
    )(a, b)


def place_tiles(slots, listed, mine, sibling):
    chips, rows, columns = sibling.shape
    per = columns // BLK
    owned = slots.shape[0] // (2 * chips)

    def body(slots_ref, listed_ref, *refs):
        mine_refs, sibling_ref = refs[:chips], refs[chips]
        outs, held = refs[chips + 1 : 2 * chips + 1], refs[2 * chips + 1]
        start = pl.multiple_of(place_on_mesh()[1] * rows, rows)
        for j in range(chips):
            held[j] = mine_refs[j][pl.ds(start, rows), :]
            held[chips + j] = sibling_ref[j]
        for r in range(chips):
            for c in range(2):
                for v in range(owned):
                    n = (r * 2 + c) * owned + v
                    slot = slots_ref[n]
                    column = pl.multiple_of(lax.rem(slot, per) * BLK, BLK)
                    tile = held[slot // per, :, pl.ds(column, BLK)]
                    outs[r][c * rows : (c + 1) * rows, v * BLK : (v + 1) * BLK] = jnp.where(
                        listed_ref[n] > 0, tile, jnp.zeros_like(tile)
                    )

    shape = jax.ShapeDtypeStruct((2 * rows, owned * BLK), sibling.dtype)
    return pl.pallas_call(
        body,
        out_shape=[shape] * chips,
        in_specs=[SCALARS] * 2 + [WHOLE] * (chips + 1),
        out_specs=[WHOLE] * chips,
        scratch_shapes=[pltpu.VMEM((2 * chips, rows, columns), sibling.dtype)],
        compiler_params=pltpu.CompilerParams(vmem_limit_bytes=16 * MIB),
        cost_estimate=cost(0, (sibling, sibling)),
    )(slots, listed, *mine, sibling)


def logit_grads(logits, stats, mine, sibling, weight, after, parts=8):
    chips, rows, vocab_rows = sibling.shape
    tokens = logits.shape[0]
    half = chips * rows
    width = weight.shape[1]
    step = width // parts
    count = len(stats)

    def body(logits_ref, *refs):
        stats_refs, refs = refs[:count], refs[count:]
        mine_refs, refs = refs[:chips], refs[chips:]
        sibling_ref, weight_ref, refs = refs[0], refs[1], refs[2 + len(after) :]
        out_ref, own_ref, other_ref, held, held_weight, columns, sems = refs
        copies = []
        for k in range(parts):
            some = pl.ds(k * step, step)
            copies.append(
                pltpu.make_async_copy(
                    weight_ref.at[:, some], held_weight.at[:, some], sems.at[k]
                )
            )
            copies[k].start()
        top, total, mass = merge([ref[...] for ref in stats_refs])
        columns[:, 0:1] = as_column(top)
        columns[:, 1:2] = as_column(loss_scale * mass / total)
        chip, core = place_on_mesh()
        mine_start = pl.multiple_of(core * rows, rows)
        for h in range(2):
            for j in range(chips):
                start = ((chip ^ j) * 2 + (core ^ h)) * rows
                part = pl.ds(pl.multiple_of(start, rows), rows)
                tiles = sibling_ref[j] if h else mine_refs[j][pl.ds(mine_start, rows), :]
                grads = (
                    columns[part, 1:2] * jnp.exp(logits_ref[part, :] - columns[part, 0:1])
                    - loss_scale * tiles.astype(jnp.float32)
                ).astype(held.dtype)
                held[(h * chips + j) * rows : (h * chips + j + 1) * rows] = grads
        for k in range(parts):
            copies[k].wait()
            some = slice(k * step, (k + 1) * step)
            share = jnp.dot(held[...], held_weight[:, some], preferred_element_type=jnp.float32)
            own_ref[:, some] = share[:half]
            other_ref[:, some] = share[half:].astype(other_ref.dtype)
        out_ref[...] = held[...].T

    ops = (logits, *stats, *mine, sibling, in_hbm(weight))
    return pl.pallas_call(
        body,
        out_shape=[
            jax.ShapeDtypeStruct((vocab_rows, tokens), jnp.bfloat16),
            jax.ShapeDtypeStruct((half, width), jnp.float32),
            jax.ShapeDtypeStruct((half, width), jnp.bfloat16),
        ],
        in_specs=[WHOLE] * (len(ops) - 1) + [ANY] * (1 + len(after)),
        out_specs=[WHOLE] * 3,
        scratch_shapes=[
            pltpu.VMEM((tokens, vocab_rows), jnp.bfloat16),
            pltpu.VMEM(weight.shape, weight.dtype),
            pltpu.VMEM((tokens, 128), jnp.float32),
            pltpu.SemaphoreType.DMA((parts,)),
        ],
        compiler_params=pltpu.CompilerParams(vmem_limit_bytes=32 * MIB),
        cost_estimate=cost(2 * weight.size * tokens, ops),
    )(*ops, *after)


def weight_grad(grads, own_cols, other_cols):
    counts = [len(parts) for parts in grads]
    flat = [part for parts in grads for part in parts]
    groups = len(grads)
    vocab_rows = sum(part.shape[0] for part in grads[0])
    half, columns = own_cols[0].shape

    def body(*refs):
        own_refs, other_refs = refs[len(flat) : -1][:groups], refs[len(flat) : -1][groups:]
        out_ref = refs[-1]
        total = None
        for r in range(groups):
            at = sum(counts[:r])
            parts = [ref[...] for ref in refs[at : at + counts[r]]]
            rows = jnp.concatenate(parts) if counts[r] > 1 else parts[0]
            for n, ref in enumerate((own_refs[r], other_refs[r])):
                term = jnp.dot(
                    rows[:, n * half : (n + 1) * half], ref[...], preferred_element_type=jnp.float32
                )
                total = term if total is None else total + term
        out_ref[...] = total.astype(out_ref.dtype)

    ops = [*flat, *own_cols, *other_cols]
    return pl.pallas_call(
        body,
        out_shape=jax.ShapeDtypeStruct((vocab_rows, columns), jnp.bfloat16),
        in_specs=[WHOLE] * len(ops),
        out_specs=WHOLE,
        compiler_params=pltpu.CompilerParams(vmem_limit_bytes=24 * MIB),
        cost_estimate=cost(2 * groups * vocab_rows * 2 * half * columns, ops),
    )(*ops)


def shards(hidden, weight, teacher, block_ids):
    vocab_size = lax.axis_size("vocab")
    data_size = lax.axis_size("dp")
    rows, width = hidden.shape
    owned_blocks = weight.shape[0] // BLK
    chips = vocab_size // 2
    me = lax.axis_index("vocab")
    chip, core = place_on_mesh()

    pieces = [hidden]
    while 2 * len(pieces) < chips:
        pieces = pieces + [swap(piece, "vocab", 2 * len(pieces)) for piece in pieces]
    far = swap(hidden, "vocab", 2 * len(pieces))

    def between_chips(parts):
        return [parts[0]] + [swap(parts[r], "vocab", 2 * r) for r in range(1, chips)]

    def between_cores(parts):
        given = [lax.dynamic_slice_in_dim(part, (1 - core) * rows, rows) for part in parts]
        return swap(jnp.stack(given), "vocab", 1)

    far, late_teacher = lax.optimization_barrier((far, teacher))
    pieces = pieces + [far] + [swap(far, "vocab", 2 * j) for j in range(1, len(pieces))]
    own = jnp.concatenate(pieces)
    other = swap(own, "vocab", 1)
    got = between_chips(
        [lax.dynamic_slice_in_dim(late_teacher, (chip ^ r) * 2 * rows, 2 * rows) for r in range(chips)]
    )
    my_ids = lax.dynamic_index_in_dim(block_ids, me * rows // BLK, keepdims=False)
    per = teacher.shape[1] // BLK
    owners = jnp.stack([(chip ^ r) * 2 + c for r in range(chips) for c in range(2)])
    blocks = (owners[:, None] * owned_blocks + jnp.arange(owned_blocks)[None, :]).reshape(-1)
    match = my_ids[None, :] == blocks[:, None]
    listed = jnp.any(match, axis=1).astype(jnp.int32)
    slots = jnp.argmax(match, axis=1).astype(jnp.int32)
    source = slots // per
    place = ((source % 2) ^ core) * chips + ((source // 2) ^ chip)
    placed = place_tiles(place * per + slots % per, listed, got, between_cores(got))
    tiles = between_chips(placed)

    mass = jnp.sum(teacher, axis=1, dtype=jnp.float32)[None, :]
    logits, stats, *cols = logits_and_stats(
        own, other, rows, weight, mass, width // data_size
    )

    tiles, stats = lax.optimization_barrier((tiles, stats))
    stats = merge_pair(stats, swap(stats, "vocab", 1))
    *cols, stats = lax.optimization_barrier((*cols, stats))
    own_cols = [cols[0]] + [swap(cols[r], "dp", r) for r in range(1, data_size)]
    other_cols = [swap(x, "vocab", 1) for x in own_cols]
    bits = 2
    while 2 * bits < vocab_size:
        stats = merge_pair(stats, swap(stats, "vocab", bits))
        bits *= 2
    all_stats = [stats, swap(stats, "vocab", bits)]
    grad_logits, share, rest = logit_grads(
        logits, all_stats, tiles, between_cores(tiles), weight, own_cols
    )

    share = share + swap(rest, "vocab", 1).astype(jnp.float32)
    shares = [share[j * rows : (j + 1) * rows] for j in range(chips)]
    count = 1
    while count < chips:
        for base in range(0, chips, 2 * count):
            sent = swap(shares[base + count].astype(jnp.bfloat16), "vocab", 2 * count)
            shares[base] = shares[base] + sent.astype(jnp.float32)
        count *= 2

    middle = grad_logits.shape[0] // 2
    all_grads = [[grad_logits]]
    bits = 1
    while bits < data_size:
        known = [jnp.concatenate(parts) if len(parts) > 1 else parts[0] for parts in all_grads]
        all_grads.append([swap(grad_logits, "dp", bits)])
        for r in range(1, bits):
            near, far = known[r], all_grads[bits][0]
            all_grads.append([swap(near[:middle], "dp", bits), swap(far[middle:], "dp", r)])
        bits *= 2
    grad_weight = weight_grad(all_grads, own_cols, other_cols)
    return (shares[0].astype(jnp.bfloat16), grad_weight)


def solution(mesh):
    placed = (P(("dp", "vocab"), None), P("vocab", None), P("dp", "vocab"), P("dp", None))

    def run(hidden, weight, teacher, block_ids):
        rows = hidden.shape[0] // (mesh.shape["dp"] * mesh.shape["vocab"])
        paired = all(size & (size - 1) == 0 for size in mesh.shape.values())
        form = shards if paired and rows % TILE_ROWS == 0 else plain_shards
        return jax.shard_map(
            form,
            mesh=mesh,
            in_specs=placed,
            out_specs=(P(("dp", "vocab"), None), P("vocab", "dp")),
            check_vma=False,
        )(hidden, weight, teacher, block_ids)

    return run
```

```python
import jax
import jax.numpy as jnp
from jax import lax
from jax.experimental import pallas as pl
from jax.experimental.pallas import tpu as pltpu
from jax.sharding import PartitionSpec as P

BLK = 128
TILE_ROWS = 16


loss_scale = 1024.0


def plain_shards(hidden, weight, teacher, block_ids):
    vocab_rows = weight.shape[0]
    owned_blocks = vocab_rows // BLK
    vocab_pos = lax.axis_index("vocab")
    full_hidden = lax.all_gather(hidden, "vocab", axis=0, tiled=True)
    token_count = full_hidden.shape[0]
    width = full_hidden.shape[1]
    logits = lax.dot_general(
        full_hidden, weight, (((1,), (1,)), ((), ())), preferred_element_type=jnp.float32
    )
    row_top = lax.pmax(jnp.max(logits, axis=1), "vocab")
    exp_terms = jnp.exp(logits - row_top[:, None])
    row_total = lax.psum(jnp.sum(exp_terms, axis=1), "vocab")
    block_count = token_count // BLK
    first_block = vocab_pos * owned_blocks
    block_range = jnp.arange(owned_blocks, dtype=jnp.int32)
    tile_cols = lax.all_gather(teacher, "vocab", axis=1, tiled=True)
    slot_count = tile_cols.shape[1] // BLK
    owned = block_ids - first_block
    onehot = (owned[:, :, None] == block_range[None, None, :]).astype(jnp.bfloat16)
    shaped = tile_cols.reshape(block_count, BLK, slot_count, BLK)
    target = jnp.einsum("bkv,btkc->btvc", onehot, shaped, preferred_element_type=jnp.float32)
    row_mass = jnp.sum(tile_cols, axis=1, dtype=jnp.float32)
    target = target.reshape(token_count, vocab_rows)
    grad_logits = (
        loss_scale * (row_mass[:, None] * (exp_terms / row_total[:, None]) - target)
    ).astype(jnp.bfloat16)
    grad_hidden = lax.psum_scatter(
        jnp.dot(grad_logits, weight, preferred_element_type=jnp.float32),
        "vocab",
        scatter_dimension=0,
        tiled=True,
    ).astype(jnp.bfloat16)
    data_count = lax.axis_size("dp")
    quarter = width // data_count
    split_hidden = full_hidden.reshape(token_count, data_count, quarter)
    quarter_rows = lax.all_to_all(
        split_hidden, "dp", split_axis=1, concat_axis=0, tiled=True
    ).reshape(token_count * data_count, quarter)
    grad_weight = lax.dot_general(
        lax.all_gather(grad_logits, "dp", axis=0, tiled=True),
        quarter_rows,
        (((0,), (0,)), ((), ())),
        preferred_element_type=jnp.float32,
    ).astype(jnp.bfloat16)
    return (grad_hidden, grad_weight)


def swap(x, axis, bits):
    return lax.ppermute(x, axis, [(i, i ^ bits) for i in range(lax.axis_size(axis))])


ANY = pl.BlockSpec(memory_space=pl.ANY)
WHOLE = pl.BlockSpec(memory_space=pltpu.VMEM)
SCALARS = pl.BlockSpec(memory_space=pltpu.SMEM)
MIB = 2**20


def in_hbm(x):
    return pltpu.with_memory_space_constraint(x, pltpu.HBM)


def place_on_mesh():
    me = lax.axis_index("vocab")
    return me // 2, lax.rem(me, 2)


def as_row(column):
    n = column.shape[0]
    same = lax.broadcasted_iota(jnp.int32, (n, n), 0) == lax.broadcasted_iota(jnp.int32, (n, n), 1)
    return jnp.sum(jnp.where(same, column, 0.0), axis=0, keepdims=True)


def as_column(row):
    n = row.shape[1]
    same = lax.broadcasted_iota(jnp.int32, (n, n), 0) == lax.broadcasted_iota(jnp.int32, (n, n), 1)
    return jnp.sum(jnp.where(same, row, 0.0), axis=1, keepdims=True)


def merge(stats):
    top = stats[0][0:1]
    for x in stats[1:]:
        top = jnp.maximum(top, x[0:1])
    total = sum(x[1:2] * jnp.exp(x[0:1] - top) for x in stats)
    mass = sum(x[2:3] for x in stats)
    return top, total, mass


def cost(flops, ops):
    return pl.CostEstimate(
        flops=flops, bytes_accessed=sum(op.size * 2 for op in ops), transcendentals=0
    )


def logits_and_stats(own, other, rows, weight, mass, parts=8, ahead=4):
    half, width = own.shape
    chips = half // rows
    tokens = 2 * half
    vocab_rows = weight.shape[0]
    step = vocab_rows // parts

    def body(*refs):
        piece_refs, refs = refs[:2], refs[2:]
        weight_ref, mass_ref, out_ref, stats_ref, refs = *refs[:4], refs[4:]
        held, held_weight, sems, piece_sems = refs
        chip, core = place_on_mesh()
        loads = []
        for h in range(2):
            for j in range(chips):
                start = ((chip ^ j) * 2 + (core ^ h)) * rows
                n = h * chips + j
                loads.append(
                    pltpu.make_async_copy(
                        piece_refs[h].at[pl.ds(j * rows, rows)],
                        held.at[pl.ds(pl.multiple_of(start, rows), rows)],
                        piece_sems.at[n],
                    )
                )
                loads[n].start()
        copies = []
        for k in range(parts):
            some = pl.ds(k * step, step)
            copies.append(
                pltpu.make_async_copy(weight_ref.at[some], held_weight.at[some], sems.at[k])
            )
        for k in range(ahead):
            copies[k].start()
        for load in loads:
            load.wait()
        for k in range(parts):
            copies[k].wait()
            if k + ahead < parts:
                copies[k + ahead].start()
            if (k + 1) % ahead == 0:
                some = slice((k + 1 - ahead) * step, (k + 1) * step)
                out_ref[:, some] = lax.dot_general(
                    held[...],
                    held_weight[some],
                    (((1,), (1,)), ((), ())),
                    preferred_element_type=jnp.float32,
                )
        top = jnp.max(out_ref[...], axis=1, keepdims=True)
        total = jnp.sum(jnp.exp(out_ref[...] - top), axis=1, keepdims=True)
        stats_ref[0:1] = as_row(top)
        stats_ref[1:2] = as_row(total)
        stats_ref[2:3] = mass_ref[...]
        stats_ref[3:8] = jnp.zeros((5, tokens), jnp.float32)

    ops = [own, other, in_hbm(weight), mass]
    return pl.pallas_call(
        body,
        out_shape=[
            jax.ShapeDtypeStruct((tokens, vocab_rows), jnp.float32),
            jax.ShapeDtypeStruct((8, tokens), jnp.float32),
        ],
        in_specs=[ANY] * 3 + [WHOLE],
        out_specs=[WHOLE, WHOLE],
        scratch_shapes=[
            pltpu.VMEM((tokens, width), weight.dtype),
            pltpu.VMEM(weight.shape, weight.dtype),
            pltpu.SemaphoreType.DMA((parts,)),
            pltpu.SemaphoreType.DMA((2 * chips,)),
        ],
        compiler_params=pltpu.CompilerParams(vmem_limit_bytes=32 * MIB),
        cost_estimate=cost(2 * tokens * weight.size, ops),
    )(*ops)


def cut_columns(own, quarter):
    groups = own.shape[1] // quarter

    def body(own_ref, *refs):
        outs, sems = refs[:groups], refs[groups]
        data_pos = lax.axis_index("dp")
        moves = []
        for r in range(groups):
            column = pl.multiple_of((data_pos ^ r) * quarter, quarter)
            moves.append(
                pltpu.make_async_copy(own_ref.at[:, pl.ds(column, quarter)], outs[r], sems.at[r])
            )
            moves[r].start()
        for move in moves:
            move.wait()

    return pl.pallas_call(
        body,
        out_shape=[jax.ShapeDtypeStruct((own.shape[0], quarter), own.dtype)] * groups,
        in_specs=[ANY],
        out_specs=[ANY] * groups,
        scratch_shapes=[pltpu.SemaphoreType.DMA((groups,))],
        compiler_params=pltpu.CompilerParams(vmem_limit_bytes=MIB),
        cost_estimate=cost(0, (own,)),
    )(own)


def merge_pair(a, b, after=()):
    def body(a_ref, b_ref, *refs):
        out_ref = refs[-1]
        for k, row in enumerate(merge([a_ref[...], b_ref[...]])):
            out_ref[k : k + 1] = row
        out_ref[3:8] = jnp.zeros((5, a.shape[1]), jnp.float32)

    return pl.pallas_call(
        body,
        out_shape=jax.ShapeDtypeStruct(a.shape, a.dtype),
        in_specs=[WHOLE, WHOLE] + [ANY] * len(after),
        out_specs=WHOLE,
        compiler_params=pltpu.CompilerParams(vmem_limit_bytes=MIB),
        cost_estimate=cost(0, (a, b)),
    )(a, b, *after)


def siblings_part_after(parts, rows, after):
    def body(*refs):
        start = pl.multiple_of((1 - place_on_mesh()[1]) * rows, rows)
        for j in range(len(parts)):
            refs[-1][j] = refs[j][pl.ds(start, rows), :]

    return pl.pallas_call(
        body,
        out_shape=jax.ShapeDtypeStruct((len(parts), rows, parts[0].shape[1]), parts[0].dtype),
        in_specs=[WHOLE] * len(parts) + [ANY] * len(after),
        out_specs=WHOLE,
        compiler_params=pltpu.CompilerParams(vmem_limit_bytes=4 * MIB),
        cost_estimate=cost(0, parts),
    )(*parts, *after)


def place_tiles(slots, listed, mine, sibling):
    chips, rows, columns = sibling.shape
    per = columns // BLK
    owned = slots.shape[0] // (2 * chips)

    def body(slots_ref, listed_ref, *refs):
        mine_refs, sibling_ref = refs[:chips], refs[chips]
        outs, held = refs[chips + 1 : 2 * chips + 1], refs[2 * chips + 1]
        start = pl.multiple_of(place_on_mesh()[1] * rows, rows)
        for j in range(chips):
            held[j] = mine_refs[j][pl.ds(start, rows), :]
            held[chips + j] = sibling_ref[j]
        for r in range(chips):
            for c in range(2):
                for v in range(owned):
                    n = (r * 2 + c) * owned + v
                    slot = slots_ref[n]
                    column = pl.multiple_of(lax.rem(slot, per) * BLK, BLK)
                    tile = held[slot // per, :, pl.ds(column, BLK)]
                    outs[r][c * rows : (c + 1) * rows, v * BLK : (v + 1) * BLK] = jnp.where(
                        listed_ref[n] > 0, tile, jnp.zeros_like(tile)
                    )

    shape = jax.ShapeDtypeStruct((2 * rows, owned * BLK), sibling.dtype)
    return pl.pallas_call(
        body,
        out_shape=[shape] * chips,
        in_specs=[SCALARS] * 2 + [WHOLE] * (chips + 1),
        out_specs=[WHOLE] * chips,
        scratch_shapes=[pltpu.VMEM((2 * chips, rows, columns), sibling.dtype)],
        compiler_params=pltpu.CompilerParams(vmem_limit_bytes=16 * MIB),
        cost_estimate=cost(0, (sibling, sibling)),
    )(slots, listed, *mine, sibling)


def logit_grads(logits, stats, mine, sibling, weight, cols, parts=8):
    chips, rows, vocab_rows = sibling.shape
    tokens = logits.shape[0]
    half = chips * rows
    width = weight.shape[1]
    step = width // parts
    count = len(stats)

    def body(logits_ref, *refs):
        stats_refs, refs = refs[:count], refs[count:]
        mine_refs, refs = refs[:chips], refs[chips:]
        sibling_ref, weight_ref, refs = refs[0], refs[1], refs[2:]
        cols_refs, refs = refs[: len(cols)], refs[len(cols) :]
        out_ref, own_ref, other_ref, stacked_ref, held_weight, columns, sems, cols_sems = refs
        moves = [
            pltpu.make_async_copy(ref, stacked_ref.at[r], cols_sems.at[r])
            for r, ref in enumerate(cols_refs)
        ]
        copies = []
        for k in range(parts):
            some = pl.ds(k * step, step)
            copies.append(
                pltpu.make_async_copy(
                    weight_ref.at[:, some], held_weight.at[:, some], sems.at[k]
                )
            )
            copies[k].start()
        for move in moves:
            move.start()
        top, total, mass = merge([ref[...] for ref in stats_refs])
        columns[:, 0:1] = as_column(top)
        columns[:, 1:2] = as_column(loss_scale * mass / total)
        chip, core = place_on_mesh()
        mine_start = pl.multiple_of(core * rows, rows)
        for h in range(2):
            for j in range(chips):
                start = ((chip ^ j) * 2 + (core ^ h)) * rows
                part = pl.ds(pl.multiple_of(start, rows), rows)
                tiles = sibling_ref[j] if h else mine_refs[j][pl.ds(mine_start, rows), :]
                grads = (
                    columns[part, 1:2] * jnp.exp(logits_ref[part, :] - columns[part, 0:1])
                    - loss_scale * tiles.astype(jnp.float32)
                ).astype(out_ref.dtype)
                out_ref[(h * chips + j) * rows : (h * chips + j + 1) * rows] = grads
        for k in range(parts):
            copies[k].wait()
            some = slice(k * step, (k + 1) * step)
            share = jnp.dot(out_ref[...], held_weight[:, some], preferred_element_type=jnp.float32)
            own_ref[:, some] = share[:half]
            other_ref[:, some] = share[half:].astype(other_ref.dtype)
        for move in moves:
            move.wait()

    ops = (logits, *stats, *mine, sibling, in_hbm(weight))
    return pl.pallas_call(
        body,
        out_shape=[
            jax.ShapeDtypeStruct((tokens, vocab_rows), jnp.bfloat16),
            jax.ShapeDtypeStruct((half, width), jnp.float32),
            jax.ShapeDtypeStruct((half, width), jnp.bfloat16),
            jax.ShapeDtypeStruct((len(cols), *cols[0].shape), cols[0].dtype),
        ],
        in_specs=[WHOLE] * (len(ops) - 1) + [ANY] * (1 + len(cols)),
        out_specs=[WHOLE] * 3 + [ANY],
        scratch_shapes=[
            pltpu.VMEM(weight.shape, weight.dtype),
            pltpu.VMEM((tokens, 128), jnp.float32),
            pltpu.SemaphoreType.DMA((parts,)),
            pltpu.SemaphoreType.DMA((len(cols),)),
        ],
        compiler_params=pltpu.CompilerParams(vmem_limit_bytes=32 * MIB),
        cost_estimate=cost(2 * weight.size * tokens, ops),
    )(*ops, *cols)


def weight_grad(grads, own_cols, other_cols, after):
    flat = [part for parts in grads for part in parts]
    vocab_rows = flat[0].shape[1]
    columns = own_cols.shape[2]
    tokens = sum(part.shape[0] for part in flat)

    def body(*refs):
        rows = jnp.concatenate([ref[...] for ref in refs[: len(flat)]])
        cols_refs = refs[len(flat) : len(flat) + 2]
        cols = jnp.concatenate([ref[r] for r in range(own_cols.shape[0]) for ref in cols_refs])
        refs[-1][...] = lax.dot_general(
            rows, cols, (((0,), (0,)), ((), ())), preferred_element_type=jnp.float32
        ).astype(refs[-1].dtype)

    ops = [*flat, own_cols, other_cols]
    return pl.pallas_call(
        body,
        out_shape=jax.ShapeDtypeStruct((vocab_rows, columns), jnp.bfloat16),
        in_specs=[WHOLE] * len(ops) + [ANY] * len(after),
        out_specs=WHOLE,
        compiler_params=pltpu.CompilerParams(vmem_limit_bytes=24 * MIB),
        cost_estimate=cost(2 * tokens * vocab_rows * columns, ops),
    )(*ops, *after)


def shards(hidden, weight, teacher, block_ids):
    vocab_size = lax.axis_size("vocab")
    data_size = lax.axis_size("dp")
    rows, width = hidden.shape
    owned_blocks = weight.shape[0] // BLK
    chips = vocab_size // 2
    me = lax.axis_index("vocab")
    chip, core = place_on_mesh()

    pieces = [hidden]
    while 2 * len(pieces) < chips:
        pieces = pieces + [swap(piece, "vocab", 2 * len(pieces)) for piece in pieces]
    far = swap(hidden, "vocab", 2 * len(pieces))

    def between_chips(parts):
        return [parts[0]] + [swap(parts[r], "vocab", 2 * r) for r in range(1, chips)]

    def siblings_part(parts):
        given = [lax.dynamic_slice_in_dim(part, (1 - core) * rows, rows) for part in parts]
        return jnp.stack(given)

    pieces = pieces + [far] + [swap(far, "vocab", 2 * j) for j in range(1, len(pieces))]
    got = between_chips(
        [lax.dynamic_slice_in_dim(teacher, (chip ^ r) * 2 * rows, 2 * rows) for r in range(chips)]
    )
    pieces, got = lax.optimization_barrier((pieces, got))
    own = jnp.concatenate(pieces)
    other = swap(own, "vocab", 1)
    my_ids = lax.dynamic_index_in_dim(block_ids, me * rows // BLK, keepdims=False)
    per = teacher.shape[1] // BLK
    owners = jnp.stack([(chip ^ r) * 2 + c for r in range(chips) for c in range(2)])
    blocks = (owners[:, None] * owned_blocks + jnp.arange(owned_blocks)[None, :]).reshape(-1)
    match = my_ids[None, :] == blocks[:, None]
    listed = jnp.any(match, axis=1).astype(jnp.int32)
    slots = jnp.argmax(match, axis=1).astype(jnp.int32)
    source = slots // per
    place = ((source % 2) ^ core) * chips + ((source // 2) ^ chip)
    placed = place_tiles(
        place * per + slots % per, listed, got, swap(siblings_part(got), "vocab", 1)
    )
    tiles = between_chips(placed)

    mass = jnp.sum(teacher, axis=1, dtype=jnp.float32)[None, :]
    logits, stats = logits_and_stats(own, other, rows, weight, mass)

    cols = cut_columns(own, width // data_size)
    own_cols = [cols[0]] + [swap(cols[r], "dp", r) for r in range(1, data_size)]

    stats = merge_pair(stats, swap(stats, "vocab", 1))
    bits = 2
    while 2 * bits < vocab_size:
        stats = merge_pair(stats, swap(stats, "vocab", bits))
        bits *= 2
    all_stats = [stats, swap(stats, "vocab", bits)]
    other_tiles = swap(siblings_part_after(tiles, rows, [stats]), "vocab", 1)
    grad_logits, share, rest, own_cols = logit_grads(
        logits, all_stats, tiles, other_tiles, weight, own_cols
    )
    other_cols = swap(own_cols, "vocab", 1)

    share = share + swap(rest, "vocab", 1).astype(jnp.float32)
    shares = [share[j * rows : (j + 1) * rows] for j in range(chips)]
    count = 1
    while count < chips:
        for base in range(chips - 2 * count, -1, -2 * count):
            sent = swap(shares[base + count].astype(jnp.bfloat16), "vocab", 2 * count)
            shares[base] = shares[base] + sent.astype(jnp.float32)
        count *= 2

    middle = grad_logits.shape[0] // 2
    all_grads = [[grad_logits]]
    bits = 1
    while bits < data_size:
        known = [jnp.concatenate(parts) if len(parts) > 1 else parts[0] for parts in all_grads]
        all_grads.append([swap(grad_logits, "dp", bits)])
        for r in range(1, bits):
            near, far = known[r], all_grads[bits][0]
            all_grads.append([swap(near[:middle], "dp", bits), swap(far[middle:], "dp", r)])
        bits *= 2
    grad_weight = weight_grad(all_grads, own_cols, other_cols, [shares[0]])
    return (shares[0].astype(jnp.bfloat16), grad_weight)


def solution(mesh):
    placed = (P(("dp", "vocab"), None), P("vocab", None), P("dp", "vocab"), P("dp", None))

    def run(hidden, weight, teacher, block_ids):
        rows = hidden.shape[0] // (mesh.shape["dp"] * mesh.shape["vocab"])
        paired = all(size & (size - 1) == 0 for size in mesh.shape.values())
        form = shards if paired and rows % TILE_ROWS == 0 else plain_shards
        return jax.shard_map(
            form,
            mesh=mesh,
            in_specs=placed,
            out_specs=(P(("dp", "vocab"), None), P("vocab", "dp")),
            check_vma=False,
        )(hidden, weight, teacher, block_ids)

    return run
```

```python
import jax
import jax.numpy as jnp
from jax import lax
from jax.experimental import pallas as pl
from jax.experimental.pallas import tpu as pltpu
from jax.sharding import PartitionSpec as P

BLK = 128
TILE_ROWS = 16
CORES = 2


loss_scale = 1024.0


def plain_shards(hidden, weight, teacher, block_ids):
    vocab_rows = weight.shape[0]
    owned_blocks = vocab_rows // BLK
    vocab_pos = lax.axis_index("vocab")
    full_hidden = lax.all_gather(hidden, "vocab", axis=0, tiled=True)
    token_count = full_hidden.shape[0]
    width = full_hidden.shape[1]
    logits = lax.dot_general(
        full_hidden, weight, (((1,), (1,)), ((), ())), preferred_element_type=jnp.float32
    )
    row_top = lax.pmax(jnp.max(logits, axis=1), "vocab")
    exp_terms = jnp.exp(logits - row_top[:, None])
    row_total = lax.psum(jnp.sum(exp_terms, axis=1), "vocab")
    block_count = token_count // BLK
    first_block = vocab_pos * owned_blocks
    block_range = jnp.arange(owned_blocks, dtype=jnp.int32)
    tile_cols = lax.all_gather(teacher, "vocab", axis=1, tiled=True)
    slot_count = tile_cols.shape[1] // BLK
    owned = block_ids - first_block
    onehot = (owned[:, :, None] == block_range[None, None, :]).astype(jnp.bfloat16)
    shaped = tile_cols.reshape(block_count, BLK, slot_count, BLK)
    target = jnp.einsum("bkv,btkc->btvc", onehot, shaped, preferred_element_type=jnp.float32)
    row_mass = jnp.sum(tile_cols, axis=1, dtype=jnp.float32)
    target = target.reshape(token_count, vocab_rows)
    grad_logits = (
        loss_scale * (row_mass[:, None] * (exp_terms / row_total[:, None]) - target)
    ).astype(jnp.bfloat16)
    grad_hidden = lax.psum_scatter(
        jnp.dot(grad_logits, weight, preferred_element_type=jnp.float32),
        "vocab",
        scatter_dimension=0,
        tiled=True,
    ).astype(jnp.bfloat16)
    data_count = lax.axis_size("dp")
    quarter = width // data_count
    split_hidden = full_hidden.reshape(token_count, data_count, quarter)
    quarter_rows = lax.all_to_all(
        split_hidden, "dp", split_axis=1, concat_axis=0, tiled=True
    ).reshape(token_count * data_count, quarter)
    grad_weight = lax.dot_general(
        lax.all_gather(grad_logits, "dp", axis=0, tiled=True),
        quarter_rows,
        (((0,), (0,)), ((), ())),
        preferred_element_type=jnp.float32,
    ).astype(jnp.bfloat16)
    return (grad_hidden, grad_weight)


def swap(x, axis, bits):
    return lax.ppermute(x, axis, [(i, i ^ bits) for i in range(lax.axis_size(axis))])


ANY = pl.BlockSpec(memory_space=pl.ANY)
WHOLE = pl.BlockSpec(memory_space=pltpu.VMEM)
SCALARS = pl.BlockSpec(memory_space=pltpu.SMEM)
MIB = 2**20


def in_hbm(x):
    return pltpu.with_memory_space_constraint(x, pltpu.HBM)


def place_on_mesh():
    me = lax.axis_index("vocab")
    return me // 2, lax.rem(me, 2)


def as_row(column):
    n = column.shape[0]
    same = lax.broadcasted_iota(jnp.int32, (n, n), 0) == lax.broadcasted_iota(jnp.int32, (n, n), 1)
    return jnp.sum(jnp.where(same, column, 0.0), axis=0, keepdims=True)


def as_column(row):
    n = row.shape[1]
    same = lax.broadcasted_iota(jnp.int32, (n, n), 0) == lax.broadcasted_iota(jnp.int32, (n, n), 1)
    return jnp.sum(jnp.where(same, row, 0.0), axis=1, keepdims=True)


def merge(stats):
    top = stats[0][0:1]
    for x in stats[1:]:
        top = jnp.maximum(top, x[0:1])
    total = sum(x[1:2] * jnp.exp(x[0:1] - top) for x in stats)
    mass = sum(x[2:3] for x in stats)
    return top, total, mass


def cost(flops, ops):
    return pl.CostEstimate(
        flops=flops, bytes_accessed=sum(op.size * 2 for op in ops), transcendentals=0
    )


def logits_and_stats(own, other, rows, weight, mass, quarter, parts=8, ahead=4):
    half, width = own.shape
    chips = half // rows
    tokens = 2 * half
    vocab_rows = weight.shape[0]
    step = vocab_rows // parts

    def body(*refs):
        piece_refs, refs = refs[:2], refs[2:]
        weight_ref, mass_ref, out_ref, stats_ref, refs = *refs[:4], refs[4:]
        kept_ref, near_ref, far_ref, held, held_weight, sems, piece_sems, cols_sems = refs
        chip, core = place_on_mesh()
        data_pos = lax.axis_index("dp")
        stores = []

        def store(h, group, target):
            column = pl.multiple_of(group * quarter, quarter)
            stores.append(
                pltpu.make_async_copy(
                    piece_refs[h].at[:, pl.ds(column, quarter)], target, cols_sems.at[len(stores)]
                )
            )
            stores[-1].start()

        loads = []
        for h in range(2):
            for j in range(chips):
                start = ((chip ^ j) * 2 + (core ^ h)) * rows
                n = h * chips + j
                loads.append(
                    pltpu.make_async_copy(
                        piece_refs[h].at[pl.ds(j * rows, rows)],
                        held.at[pl.ds(pl.multiple_of(start, rows), rows)],
                        piece_sems.at[n],
                    )
                )
                loads[n].start()
        copies = []
        for k in range(parts):
            some = pl.ds(k * step, step)
            copies.append(
                pltpu.make_async_copy(weight_ref.at[some], held_weight.at[some], sems.at[k])
            )
        for k in range(ahead):
            copies[k].start()
        for h in range(2):
            part = pl.ds(pl.multiple_of((core ^ h) * half, half), half)
            store(h, data_pos ^ (core + 1), near_ref.at[part])
            store(h, data_pos, kept_ref.at[part])
        store(0, data_pos ^ 3, far_ref)
        for load in loads:
            load.wait()
        for k in range(parts):
            copies[k].wait()
            if k + ahead < parts:
                copies[k + ahead].start()
            if (k + 1) % ahead == 0:
                some = slice((k + 1 - ahead) * step, (k + 1) * step)
                values = lax.dot_general(
                    held[...],
                    held_weight[some],
                    (((1,), (1,)), ((), ())),
                    preferred_element_type=jnp.float32,
                )
                out_ref[:, some] = values
                part_top = jnp.max(values, axis=1, keepdims=True)
                part_total = jnp.sum(jnp.exp(values - part_top), axis=1, keepdims=True)
                if k + 1 == ahead:
                    top, total = part_top, part_total
                else:
                    new_top = jnp.maximum(top, part_top)
                    total = total * jnp.exp(top - new_top)
                    total = total + part_total * jnp.exp(part_top - new_top)
                    top = new_top
        stats_ref[0:1] = as_row(top)
        stats_ref[1:2] = as_row(total)
        stats_ref[2:3] = mass_ref[...]
        stats_ref[3:8] = jnp.zeros((5, tokens), jnp.float32)
        for one in stores:
            one.wait()

    both = jax.ShapeDtypeStruct((tokens, quarter), own.dtype)
    ops = [own, other, in_hbm(weight), mass]
    return pl.pallas_call(
        body,
        out_shape=[
            jax.ShapeDtypeStruct((tokens, vocab_rows), jnp.float32),
            jax.ShapeDtypeStruct((8, tokens), jnp.float32),
            both,
            both,
            jax.ShapeDtypeStruct((half, quarter), own.dtype),
        ],
        in_specs=[ANY] * 3 + [WHOLE],
        out_specs=[WHOLE, WHOLE] + [ANY] * 3,
        scratch_shapes=[
            pltpu.VMEM((tokens, width), weight.dtype),
            pltpu.VMEM(weight.shape, weight.dtype),
            pltpu.SemaphoreType.DMA((parts,)),
            pltpu.SemaphoreType.DMA((2 * chips,)),
            pltpu.SemaphoreType.DMA((5,)),
        ],
        compiler_params=pltpu.CompilerParams(vmem_limit_bytes=32 * MIB),
        cost_estimate=cost(2 * tokens * weight.size, ops),
    )(*ops)


def swap_by_core(x):
    count = lax.axis_size("vocab")
    pairs = [
        (d * count + v, (d ^ (v % 2 + 1)) * count + v)
        for d in range(lax.axis_size("dp"))
        for v in range(count)
    ]
    return lax.ppermute(x, ("dp", "vocab"), pairs)


def merge_pair(a, b, after=()):
    def body(a_ref, b_ref, *refs):
        out_ref = refs[-1]
        for k, row in enumerate(merge([a_ref[...], b_ref[...]])):
            out_ref[k : k + 1] = row
        out_ref[3:8] = jnp.zeros((5, a.shape[1]), jnp.float32)

    return pl.pallas_call(
        body,
        out_shape=jax.ShapeDtypeStruct(a.shape, a.dtype),
        in_specs=[WHOLE, WHOLE] + [ANY] * len(after),
        out_specs=WHOLE,
        compiler_params=pltpu.CompilerParams(vmem_limit_bytes=MIB),
        cost_estimate=cost(0, (a, b)),
    )(a, b, *after)


def siblings_part_after(parts, rows, after):
    def body(*refs):
        start = pl.multiple_of((1 - place_on_mesh()[1]) * rows, rows)
        for j in range(len(parts)):
            refs[-1][j] = refs[j][pl.ds(start, rows), :]

    return pl.pallas_call(
        body,
        out_shape=jax.ShapeDtypeStruct((len(parts), rows, parts[0].shape[1]), parts[0].dtype),
        in_specs=[WHOLE] * len(parts) + [ANY] * len(after),
        out_specs=WHOLE,
        compiler_params=pltpu.CompilerParams(vmem_limit_bytes=4 * MIB),
        cost_estimate=cost(0, parts),
    )(*parts, *after)


def place_tiles(slots, listed, mine, sibling):
    chips, rows, columns = sibling.shape
    per = columns // BLK
    owned = slots.shape[0] // (2 * chips)

    def body(slots_ref, listed_ref, *refs):
        mine_refs, sibling_ref = refs[:chips], refs[chips]
        outs, held = refs[chips + 1 : 2 * chips + 1], refs[2 * chips + 1]
        start = pl.multiple_of(place_on_mesh()[1] * rows, rows)
        for j in range(chips):
            held[j] = mine_refs[j][pl.ds(start, rows), :]
            held[chips + j] = sibling_ref[j]
        for r in range(chips):
            for c in range(2):
                for v in range(owned):
                    n = (r * 2 + c) * owned + v
                    slot = slots_ref[n]
                    column = pl.multiple_of(lax.rem(slot, per) * BLK, BLK)
                    tile = held[slot // per, :, pl.ds(column, BLK)]
                    outs[r][c * rows : (c + 1) * rows, v * BLK : (v + 1) * BLK] = jnp.where(
                        listed_ref[n] > 0, tile, jnp.zeros_like(tile)
                    )

    shape = jax.ShapeDtypeStruct((2 * rows, owned * BLK), sibling.dtype)
    return pl.pallas_call(
        body,
        out_shape=[shape] * chips,
        in_specs=[SCALARS] * 2 + [WHOLE] * (chips + 1),
        out_specs=[WHOLE] * chips,
        scratch_shapes=[pltpu.VMEM((2 * chips, rows, columns), sibling.dtype)],
        compiler_params=pltpu.CompilerParams(vmem_limit_bytes=16 * MIB),
        cost_estimate=cost(0, (sibling, sibling)),
    )(slots, listed, *mine, sibling)


def logit_grads(logits, stats, mine, sibling, weight, cols, after, parts=8):
    chips, rows, vocab_rows = sibling.shape
    tokens = logits.shape[0]
    half = chips * rows
    width = weight.shape[1]
    step = width // parts
    count = len(stats)

    def body(logits_ref, *refs):
        stats_refs, refs = refs[:count], refs[count:]
        mine_refs, refs = refs[:chips], refs[chips:]
        sibling_ref, weight_ref, refs = refs[0], refs[1], refs[2:]
        cols_refs, refs = refs[: len(cols)], refs[len(cols) + len(after) :]
        out_ref, own_ref, other_ref, stacked_ref, held_weight, columns, sems, cols_sems = refs
        moves = []
        for r, ref in enumerate(cols_refs):
            at = sum(x.shape[0] for x in cols[:r])
            target = stacked_ref.at[at : at + cols[r].shape[0]]
            moves.append(pltpu.make_async_copy(ref, target, cols_sems.at[r]))
        copies = []
        for k in range(parts):
            some = pl.ds(k * step, step)
            copies.append(
                pltpu.make_async_copy(
                    weight_ref.at[:, some], held_weight.at[:, some], sems.at[k]
                )
            )
            copies[k].start()
        for move in moves:
            move.start()
        top, total, mass = merge([ref[...] for ref in stats_refs])
        columns[:, 0:1] = as_column(top)
        columns[:, 1:2] = as_column(loss_scale * mass / total)
        chip, core = place_on_mesh()
        mine_start = pl.multiple_of(core * rows, rows)
        for h in range(2):
            for j in range(chips):
                start = ((chip ^ j) * 2 + (core ^ h)) * rows
                part = pl.ds(pl.multiple_of(start, rows), rows)
                tiles = sibling_ref[j] if h else mine_refs[j][pl.ds(mine_start, rows), :]
                grads = (
                    columns[part, 1:2] * jnp.exp(logits_ref[part, :] - columns[part, 0:1])
                    - loss_scale * tiles.astype(jnp.float32)
                ).astype(out_ref.dtype)
                out_ref[(h * chips + j) * rows : (h * chips + j + 1) * rows] = grads
        for k in range(parts):
            copies[k].wait()
            some = slice(k * step, (k + 1) * step)
            share = jnp.dot(out_ref[...], held_weight[:, some], preferred_element_type=jnp.float32)
            own_ref[:, some] = share[:half]
            other_ref[:, some] = share[half:].astype(other_ref.dtype)
        for move in moves:
            move.wait()

    ops = (logits, *stats, *mine, sibling, in_hbm(weight))
    return pl.pallas_call(
        body,
        out_shape=[
            jax.ShapeDtypeStruct((tokens, vocab_rows), jnp.bfloat16),
            jax.ShapeDtypeStruct((half, width), jnp.float32),
            jax.ShapeDtypeStruct((half, width), jnp.bfloat16),
            jax.ShapeDtypeStruct((sum(x.shape[0] for x in cols), cols[0].shape[1]), cols[0].dtype),
        ],
        in_specs=[WHOLE] * (len(ops) - 1) + [ANY] * (1 + len(cols) + len(after)),
        out_specs=[WHOLE] * 3 + [ANY],
        scratch_shapes=[
            pltpu.VMEM(weight.shape, weight.dtype),
            pltpu.VMEM((tokens, 128), jnp.float32),
            pltpu.SemaphoreType.DMA((parts,)),
            pltpu.SemaphoreType.DMA((len(cols),)),
        ],
        compiler_params=pltpu.CompilerParams(vmem_limit_bytes=32 * MIB),
        cost_estimate=cost(2 * weight.size * tokens, ops),
    )(*ops, *cols, *after)


def ordered_columns(kept, mine, sibling):
    tokens = kept.shape[0]
    half = tokens // 2
    first = place_on_mesh()[1] == 0
    a, b = mine[:tokens], sibling[:tokens]
    cols = []
    for group in (kept[...], jnp.where(first, a, b), jnp.where(first, b, a)):
        low, high = group[:half], group[half:]
        cols += [jnp.where(first, low, high), jnp.where(first, high, low)]
    return jnp.concatenate(cols)


def weight_grad_part(grads, kept, mine, sibling):
    vocab_rows = grads[0].shape[1]
    tokens, columns = kept.shape

    def body(*refs):
        kept_ref, mine_ref, sibling_ref, out_ref = refs[len(grads) :]
        out_ref[...] = lax.dot_general(
            jnp.concatenate([ref[...] for ref in refs[: len(grads)]]),
            ordered_columns(kept_ref, mine_ref, sibling_ref),
            (((0,), (0,)), ((), ())),
            preferred_element_type=jnp.float32,
        )

    ops = [*grads, kept, mine, sibling]
    return pl.pallas_call(
        body,
        out_shape=jax.ShapeDtypeStruct((vocab_rows, columns), jnp.float32),
        in_specs=[WHOLE] * len(ops),
        out_specs=WHOLE,
        compiler_params=pltpu.CompilerParams(vmem_limit_bytes=24 * MIB),
        cost_estimate=cost(6 * tokens * vocab_rows * columns, ops),
    )(*ops)


def weight_grad_rest(partial, grads, mine, sibling, after, parts=4):
    vocab_rows, columns = partial.shape
    step = vocab_rows // parts
    count = sum(x.shape[0] for x in grads)
    start = mine.shape[0] - count // 2

    def body(partial_ref, *refs):
        grads_refs, refs = refs[: len(grads)], refs[len(grads) :]
        mine_ref, sibling_ref, refs = refs[0], refs[1], refs[2 + len(after) :]
        out_ref, done, sems = refs
        stores = []
        rows = jnp.concatenate([ref[...] for ref in grads_refs])
        cols = jnp.concatenate([mine_ref[start:], sibling_ref[start:]])
        for k in range(parts):
            some = slice(k * step, (k + 1) * step)
            term = lax.dot_general(
                rows[:, some], cols, (((0,), (0,)), ((), ())), preferred_element_type=jnp.float32
            )
            done[some] = (partial_ref[some] + term).astype(done.dtype)
            stores.append(pltpu.make_async_copy(done.at[some], out_ref.at[some], sems.at[k]))
            stores[k].start()
        for store in stores:
            store.wait()

    ops = [partial, *grads, mine, sibling]
    return pl.pallas_call(
        body,
        out_shape=jax.ShapeDtypeStruct((vocab_rows, columns), jnp.bfloat16),
        in_specs=[WHOLE] * len(ops) + [ANY] * len(after),
        out_specs=ANY,
        scratch_shapes=[
            pltpu.VMEM(partial.shape, jnp.bfloat16),
            pltpu.SemaphoreType.DMA((parts,)),
        ],
        compiler_params=pltpu.CompilerParams(vmem_limit_bytes=16 * MIB),
        cost_estimate=cost(2 * count * vocab_rows * columns, ops),
    )(*ops, *after)


def shards(hidden, weight, teacher, block_ids):
    vocab_size = lax.axis_size("vocab")
    data_size = lax.axis_size("dp")
    rows, width = hidden.shape
    owned_blocks = weight.shape[0] // BLK
    chips = vocab_size // 2
    me = lax.axis_index("vocab")
    chip, core = place_on_mesh()

    pieces = [hidden]
    while 2 * len(pieces) < chips:
        pieces = pieces + [swap(piece, "vocab", 2 * len(pieces)) for piece in pieces]
    far = swap(hidden, "vocab", 2 * len(pieces))

    def between_chips(parts):
        return [parts[0]] + [swap(parts[r], "vocab", 2 * r) for r in range(1, chips)]

    def siblings_part(parts):
        given = [lax.dynamic_slice_in_dim(part, (1 - core) * rows, rows) for part in parts]
        return jnp.stack(given)

    pieces = pieces + [far] + [swap(far, "vocab", 2 * j) for j in range(1, len(pieces))]
    got = between_chips(
        [lax.dynamic_slice_in_dim(teacher, (chip ^ r) * 2 * rows, 2 * rows) for r in range(chips)]
    )
    pieces, got = lax.optimization_barrier((pieces, got))
    own = jnp.concatenate(pieces)
    other = swap(own, "vocab", 1)
    my_ids = lax.dynamic_index_in_dim(block_ids, me * rows // BLK, keepdims=False)
    per = teacher.shape[1] // BLK
    owners = jnp.stack([(chip ^ r) * 2 + c for r in range(chips) for c in range(2)])
    blocks = (owners[:, None] * owned_blocks + jnp.arange(owned_blocks)[None, :]).reshape(-1)
    match = my_ids[None, :] == blocks[:, None]
    listed = jnp.any(match, axis=1).astype(jnp.int32)
    slots = jnp.argmax(match, axis=1).astype(jnp.int32)
    source = slots // per
    place = ((source % 2) ^ core) * chips + ((source // 2) ^ chip)
    placed = place_tiles(
        place * per + slots % per, listed, got, swap(siblings_part(got), "vocab", 1)
    )
    tiles = between_chips(placed)

    mass = jnp.sum(teacher, axis=1, dtype=jnp.float32)[None, :]

    logits, stats, kept, near, far = logits_and_stats(
        own, other, rows, weight, mass, width // data_size
    )
    own_cols = [swap_by_core(near), swap(far, "dp", data_size - 1)]

    stats = merge_pair(stats, swap(stats, "vocab", 1))
    bits = 2
    while 2 * bits < vocab_size:
        stats = merge_pair(stats, swap(stats, "vocab", bits))
        bits *= 2
    all_stats = [stats, swap(stats, "vocab", bits)]
    other_tiles = swap(siblings_part_after(tiles, rows, [stats]), "vocab", 1)
    spare = other_tiles[0, :TILE_ROWS, :BLK]
    spare = swap(spare, "vocab", 1)
    grad_logits, share, rest, own_cols = logit_grads(
        logits, all_stats, tiles, other_tiles, weight, own_cols, [spare]
    )
    other_cols = swap(own_cols, "vocab", 1)

    share = share + swap(rest, "vocab", 1).astype(jnp.float32)
    shares = [share[j * rows : (j + 1) * rows] for j in range(chips)]
    count = 1
    while count < chips:
        for base in range(chips - 2 * count, -1, -2 * count):
            sent = swap(shares[base + count].astype(jnp.bfloat16), "vocab", 2 * count)
            shares[base] = shares[base] + sent.astype(jnp.float32)
        count *= 2
    grad_hidden = shares[0].astype(jnp.bfloat16)

    middle = grad_logits.shape[0] // 2
    near, far = swap(grad_logits, "dp", 1), swap(grad_logits, "dp", 2)
    last = [swap(near[:middle], "dp", 2), swap(far[middle:], "dp", 1)]
    partial = weight_grad_part([grad_logits, near, far], kept, own_cols, other_cols)
    grad_weight = weight_grad_rest(partial, last, own_cols, other_cols, [grad_hidden])
    return (grad_hidden, grad_weight)


def solution(mesh):
    placed = (P(("dp", "vocab"), None), P("vocab", None), P("dp", "vocab"), P("dp", None))

    def run(hidden, weight, teacher, block_ids):
        rows = hidden.shape[0] // (mesh.shape["dp"] * mesh.shape["vocab"])
        count = mesh.shape["vocab"]
        fits = count & (count - 1) == 0 and count > 2 and mesh.shape["dp"] == CORES**2
        fits = fits and rows % TILE_ROWS == 0 and BLK % rows == 0 and count * rows % (2 * BLK) == 0
        form = shards if fits else plain_shards
        return jax.shard_map(
            form,
            mesh=mesh,
            in_specs=placed,
            out_specs=(P(("dp", "vocab"), None), P("vocab", "dp")),
            check_vma=False,
        )(hidden, weight, teacher, block_ids)

    return run
```

```python
import jax
import jax.numpy as jnp
from jax import lax
from jax.experimental import pallas as pl
from jax.experimental.pallas import tpu as pltpu
from jax.sharding import PartitionSpec as P

BLK = 128
TILE_ROWS = 16
CORES = 2


loss_scale = 1024.0


def plain_shards(hidden, weight, teacher, block_ids):
    vocab_rows = weight.shape[0]
    owned_blocks = vocab_rows // BLK
    vocab_pos = lax.axis_index("vocab")
    full_hidden = lax.all_gather(hidden, "vocab", axis=0, tiled=True)
    token_count = full_hidden.shape[0]
    width = full_hidden.shape[1]
    logits = lax.dot_general(
        full_hidden, weight, (((1,), (1,)), ((), ())), preferred_element_type=jnp.float32
    )
    row_top = lax.pmax(jnp.max(logits, axis=1), "vocab")
    exp_terms = jnp.exp(logits - row_top[:, None])
    row_total = lax.psum(jnp.sum(exp_terms, axis=1), "vocab")
    block_count = token_count // BLK
    first_block = vocab_pos * owned_blocks
    block_range = jnp.arange(owned_blocks, dtype=jnp.int32)
    tile_cols = lax.all_gather(teacher, "vocab", axis=1, tiled=True)
    slot_count = tile_cols.shape[1] // BLK
    owned = block_ids - first_block
    onehot = (owned[:, :, None] == block_range[None, None, :]).astype(jnp.bfloat16)
    shaped = tile_cols.reshape(block_count, BLK, slot_count, BLK)
    target = jnp.einsum("bkv,btkc->btvc", onehot, shaped, preferred_element_type=jnp.float32)
    row_mass = jnp.sum(tile_cols, axis=1, dtype=jnp.float32)
    target = target.reshape(token_count, vocab_rows)
    grad_logits = (
        loss_scale * (row_mass[:, None] * (exp_terms / row_total[:, None]) - target)
    ).astype(jnp.bfloat16)
    grad_hidden = lax.psum_scatter(
        jnp.dot(grad_logits, weight, preferred_element_type=jnp.float32),
        "vocab",
        scatter_dimension=0,
        tiled=True,
    ).astype(jnp.bfloat16)
    data_count = lax.axis_size("dp")
    quarter = width // data_count
    split_hidden = full_hidden.reshape(token_count, data_count, quarter)
    quarter_rows = lax.all_to_all(
        split_hidden, "dp", split_axis=1, concat_axis=0, tiled=True
    ).reshape(token_count * data_count, quarter)
    grad_weight = lax.dot_general(
        lax.all_gather(grad_logits, "dp", axis=0, tiled=True),
        quarter_rows,
        (((0,), (0,)), ((), ())),
        preferred_element_type=jnp.float32,
    ).astype(jnp.bfloat16)
    return (grad_hidden, grad_weight)


def swap(x, axis, bits):
    return lax.ppermute(x, axis, [(i, i ^ bits) for i in range(lax.axis_size(axis))])


ANY = pl.BlockSpec(memory_space=pl.ANY)
WHOLE = pl.BlockSpec(memory_space=pltpu.VMEM)
SCALARS = pl.BlockSpec(memory_space=pltpu.SMEM)
MIB = 2**20


def in_hbm(x):
    return pltpu.with_memory_space_constraint(x, pltpu.HBM)


def place_on_mesh():
    me = lax.axis_index("vocab")
    return me // 2, lax.rem(me, 2)


def as_row(column):
    n = column.shape[0]
    same = lax.broadcasted_iota(jnp.int32, (n, n), 0) == lax.broadcasted_iota(jnp.int32, (n, n), 1)
    return jnp.sum(jnp.where(same, column, 0.0), axis=0, keepdims=True)


def as_column(row):
    n = row.shape[1]
    same = lax.broadcasted_iota(jnp.int32, (n, n), 0) == lax.broadcasted_iota(jnp.int32, (n, n), 1)
    return jnp.sum(jnp.where(same, row, 0.0), axis=1, keepdims=True)


def merge(stats):
    top = stats[0][0:1]
    for x in stats[1:]:
        top = jnp.maximum(top, x[0:1])
    total = sum(x[1:2] * jnp.exp(x[0:1] - top) for x in stats)
    mass = sum(x[2:3] for x in stats)
    return top, total, mass


def cost(flops, ops):
    return pl.CostEstimate(
        flops=flops, bytes_accessed=sum(op.size * 2 for op in ops), transcendentals=0
    )


def logits_and_stats(own, other, rows, weight, mass, quarter, parts=8, ahead=4):
    half, width = own.shape
    chips = half // rows
    tokens = 2 * half
    vocab_rows = weight.shape[0]
    step = vocab_rows // parts

    def body(*refs):
        piece_refs, refs = refs[:2], refs[2:]
        weight_ref, mass_ref, out_ref, stats_ref, refs = *refs[:4], refs[4:]
        kept_ref, near_ref, far_ref, held, held_weight, sems, piece_sems, cols_sems = refs
        chip, core = place_on_mesh()
        data_pos = lax.axis_index("dp")
        stores = []

        def store(h, group, target):
            column = pl.multiple_of(group * quarter, quarter)
            stores.append(
                pltpu.make_async_copy(
                    piece_refs[h].at[:, pl.ds(column, quarter)], target, cols_sems.at[len(stores)]
                )
            )
            stores[-1].start()

        loads = []
        for h in range(2):
            for j in range(chips):
                start = ((chip ^ j) * 2 + (core ^ h)) * rows
                n = h * chips + j
                loads.append(
                    pltpu.make_async_copy(
                        piece_refs[h].at[pl.ds(j * rows, rows)],
                        held.at[pl.ds(pl.multiple_of(start, rows), rows)],
                        piece_sems.at[n],
                    )
                )
                loads[n].start()
        copies = []
        for k in range(parts):
            some = pl.ds(k * step, step)
            copies.append(
                pltpu.make_async_copy(weight_ref.at[some], held_weight.at[some], sems.at[k])
            )
        for k in range(ahead):
            copies[k].start()
        for h in range(2):
            part = pl.ds(pl.multiple_of((core ^ h) * half, half), half)
            store(h, data_pos ^ (core + 1), near_ref.at[part])
            store(h, data_pos, kept_ref.at[part])
        store(0, data_pos ^ 3, far_ref)
        for load in loads:
            load.wait()
        for k in range(parts):
            copies[k].wait()
            if k + ahead < parts:
                copies[k + ahead].start()
            if (k + 1) % ahead == 0:
                some = slice((k + 1 - ahead) * step, (k + 1) * step)
                values = lax.dot_general(
                    held[...],
                    held_weight[some],
                    (((1,), (1,)), ((), ())),
                    preferred_element_type=jnp.float32,
                )
                out_ref[:, some] = values
                part_top = jnp.max(values, axis=1, keepdims=True)
                part_total = jnp.sum(jnp.exp(values - part_top), axis=1, keepdims=True)
                if k + 1 == ahead:
                    top, total = part_top, part_total
                else:
                    new_top = jnp.maximum(top, part_top)
                    total = total * jnp.exp(top - new_top)
                    total = total + part_total * jnp.exp(part_top - new_top)
                    top = new_top
        stats_ref[0:1] = as_row(top)
        stats_ref[1:2] = as_row(total)
        stats_ref[2:3] = mass_ref[...]
        stats_ref[3:8] = jnp.zeros((5, tokens), jnp.float32)
        for one in stores:
            one.wait()

    both = jax.ShapeDtypeStruct((tokens, quarter), own.dtype)
    ops = [own, other, in_hbm(weight), mass]
    return pl.pallas_call(
        body,
        out_shape=[
            jax.ShapeDtypeStruct((tokens, vocab_rows), jnp.float32),
            jax.ShapeDtypeStruct((8, tokens), jnp.float32),
            both,
            both,
            jax.ShapeDtypeStruct((half, quarter), own.dtype),
        ],
        in_specs=[ANY] * 3 + [WHOLE],
        out_specs=[WHOLE, WHOLE] + [ANY] * 3,
        scratch_shapes=[
            pltpu.VMEM((tokens, width), weight.dtype),
            pltpu.VMEM(weight.shape, weight.dtype),
            pltpu.SemaphoreType.DMA((parts,)),
            pltpu.SemaphoreType.DMA((2 * chips,)),
            pltpu.SemaphoreType.DMA((5,)),
        ],
        compiler_params=pltpu.CompilerParams(vmem_limit_bytes=32 * MIB),
        cost_estimate=cost(2 * tokens * weight.size, ops),
    )(*ops)


def swap_by_core(x):
    count = lax.axis_size("vocab")
    pairs = [
        (d * count + v, (d ^ (v % 2 + 1)) * count + v)
        for d in range(lax.axis_size("dp"))
        for v in range(count)
    ]
    return lax.ppermute(x, ("dp", "vocab"), pairs)


def merge_pair(a, b, after=()):
    def body(a_ref, b_ref, *refs):
        out_ref = refs[-1]
        for k, row in enumerate(merge([a_ref[...], b_ref[...]])):
            out_ref[k : k + 1] = row
        out_ref[3:8] = jnp.zeros((5, a.shape[1]), jnp.float32)

    return pl.pallas_call(
        body,
        out_shape=jax.ShapeDtypeStruct(a.shape, a.dtype),
        in_specs=[WHOLE, WHOLE] + [ANY] * len(after),
        out_specs=WHOLE,
        compiler_params=pltpu.CompilerParams(vmem_limit_bytes=MIB),
        cost_estimate=cost(0, (a, b)),
    )(a, b, *after)


def siblings_part_after(parts, rows, after):
    def body(*refs):
        start = pl.multiple_of((1 - place_on_mesh()[1]) * rows, rows)
        for j in range(len(parts)):
            refs[-1][j] = refs[j][pl.ds(start, rows), :]

    return pl.pallas_call(
        body,
        out_shape=jax.ShapeDtypeStruct((len(parts), rows, parts[0].shape[1]), parts[0].dtype),
        in_specs=[WHOLE] * len(parts) + [ANY] * len(after),
        out_specs=WHOLE,
        compiler_params=pltpu.CompilerParams(vmem_limit_bytes=4 * MIB),
        cost_estimate=cost(0, parts),
    )(*parts, *after)


def place_tiles(slots, listed, mine, sibling):
    chips, rows, columns = sibling.shape
    per = columns // BLK
    owned = slots.shape[0] // (2 * chips)

    def body(slots_ref, listed_ref, *refs):
        mine_refs, sibling_ref = refs[:chips], refs[chips]
        outs, held = refs[chips + 1 : 2 * chips + 1], refs[2 * chips + 1]
        start = pl.multiple_of(place_on_mesh()[1] * rows, rows)
        for j in range(chips):
            held[j] = mine_refs[j][pl.ds(start, rows), :]
            held[chips + j] = sibling_ref[j]
        for r in range(chips):
            for c in range(2):
                for v in range(owned):
                    n = (r * 2 + c) * owned + v
                    slot = slots_ref[n]
                    column = pl.multiple_of(lax.rem(slot, per) * BLK, BLK)
                    tile = held[slot // per, :, pl.ds(column, BLK)]
                    outs[r][c * rows : (c + 1) * rows, v * BLK : (v + 1) * BLK] = jnp.where(
                        listed_ref[n] > 0, tile, jnp.zeros_like(tile)
                    )

    shape = jax.ShapeDtypeStruct((2 * rows, owned * BLK), sibling.dtype)
    return pl.pallas_call(
        body,
        out_shape=[shape] * chips,
        in_specs=[SCALARS] * 2 + [WHOLE] * (chips + 1),
        out_specs=[WHOLE] * chips,
        scratch_shapes=[pltpu.VMEM((2 * chips, rows, columns), sibling.dtype)],
        compiler_params=pltpu.CompilerParams(vmem_limit_bytes=16 * MIB),
        cost_estimate=cost(0, (sibling, sibling)),
    )(slots, listed, *mine, sibling)


def logit_grads(logits, stats, mine, sibling, weight, cols, after, parts=4, ahead=3):
    chips, rows, vocab_rows = sibling.shape
    tokens = logits.shape[0]
    half = chips * rows
    width = weight.shape[1]
    step = width // parts
    count = len(stats)

    def body(logits_ref, *refs):
        stats_refs, refs = refs[:count], refs[count:]
        mine_refs, refs = refs[:chips], refs[chips:]
        sibling_ref, weight_ref, refs = refs[0], refs[1], refs[2:]
        cols_refs, refs = refs[: len(cols)], refs[len(cols) + len(after) :]
        out_ref, own_ref, other_ref, stacked_ref, held_weight, columns, sems, cols_sems = refs
        moves = []
        for r, ref in enumerate(cols_refs):
            at = sum(x.shape[0] for x in cols[:r])
            target = stacked_ref.at[at : at + cols[r].shape[0]]
            moves.append(pltpu.make_async_copy(ref, target, cols_sems.at[r]))
        copies = []
        for k in range(parts):
            some = pl.ds(k * step, step)
            copies.append(
                pltpu.make_async_copy(
                    weight_ref.at[:, some], held_weight.at[:, some], sems.at[k]
                )
            )
        for k in range(ahead):
            copies[k].start()
        for move in moves:
            move.start()
        top, total, mass = merge([ref[...] for ref in stats_refs])
        columns[:, 0:1] = as_column(top)
        columns[:, 1:2] = as_column(loss_scale * mass / total)
        chip, core = place_on_mesh()
        mine_start = pl.multiple_of(core * rows, rows)
        for h in range(2):
            for j in range(chips):
                start = ((chip ^ j) * 2 + (core ^ h)) * rows
                part = pl.ds(pl.multiple_of(start, rows), rows)
                tiles = sibling_ref[j] if h else mine_refs[j][pl.ds(mine_start, rows), :]
                grads = (
                    columns[part, 1:2] * jnp.exp(logits_ref[part, :] - columns[part, 0:1])
                    - loss_scale * tiles.astype(jnp.float32)
                ).astype(out_ref.dtype)
                out_ref[(h * chips + j) * rows : (h * chips + j + 1) * rows] = grads
        for k in range(parts):
            copies[k].wait()
            if k + ahead < parts:
                copies[k + ahead].start()
            some = slice(k * step, (k + 1) * step)
            share = jnp.dot(out_ref[...], held_weight[:, some], preferred_element_type=jnp.float32)
            own_ref[:, some] = share[:half]
            other_ref[:, some] = share[half:].astype(other_ref.dtype)
        for move in moves:
            move.wait()

    ops = (logits, *stats, *mine, sibling, in_hbm(weight))
    return pl.pallas_call(
        body,
        out_shape=[
            jax.ShapeDtypeStruct((tokens, vocab_rows), jnp.bfloat16),
            jax.ShapeDtypeStruct((half, width), jnp.float32),
            jax.ShapeDtypeStruct((half, width), jnp.bfloat16),
            jax.ShapeDtypeStruct((sum(x.shape[0] for x in cols), cols[0].shape[1]), cols[0].dtype),
        ],
        in_specs=[WHOLE] * (len(ops) - 1) + [ANY] * (1 + len(cols) + len(after)),
        out_specs=[WHOLE] * 3 + [ANY],
        scratch_shapes=[
            pltpu.VMEM(weight.shape, weight.dtype),
            pltpu.VMEM((tokens, 128), jnp.float32),
            pltpu.SemaphoreType.DMA((parts,)),
            pltpu.SemaphoreType.DMA((len(cols),)),
        ],
        compiler_params=pltpu.CompilerParams(vmem_limit_bytes=32 * MIB),
        cost_estimate=cost(2 * weight.size * tokens, ops),
    )(*ops, *cols, *after)


def ordered_columns(kept, mine, sibling):
    tokens = kept.shape[0]
    half = tokens // 2
    first = place_on_mesh()[1] == 0
    a, b = mine[:tokens], sibling[:tokens]
    cols = []
    for group in (kept[...], jnp.where(first, a, b), jnp.where(first, b, a)):
        low, high = group[:half], group[half:]
        cols += [jnp.where(first, low, high), jnp.where(first, high, low)]
    return jnp.concatenate(cols)


def weight_grad_part(grads, kept, mine, sibling):
    vocab_rows = grads[0].shape[1]
    tokens, columns = kept.shape

    def body(*refs):
        kept_ref, mine_ref, sibling_ref, out_ref = refs[len(grads) :]
        out_ref[...] = lax.dot_general(
            jnp.concatenate([ref[...] for ref in refs[: len(grads)]]),
            ordered_columns(kept_ref, mine_ref, sibling_ref),
            (((0,), (0,)), ((), ())),
            preferred_element_type=jnp.float32,
        )

    ops = [*grads, kept, mine, sibling]
    return pl.pallas_call(
        body,
        out_shape=jax.ShapeDtypeStruct((vocab_rows, columns), jnp.float32),
        in_specs=[WHOLE] * len(ops),
        out_specs=WHOLE,
        compiler_params=pltpu.CompilerParams(vmem_limit_bytes=24 * MIB),
        cost_estimate=cost(6 * tokens * vocab_rows * columns, ops),
    )(*ops)


def weight_grad_rest(partial, grads, mine, sibling, after, parts=4):
    vocab_rows, columns = partial.shape
    step = vocab_rows // parts
    count = sum(x.shape[0] for x in grads)
    start = mine.shape[0] - count // 2

    def body(partial_ref, *refs):
        grads_refs, refs = refs[: len(grads)], refs[len(grads) :]
        mine_ref, sibling_ref, refs = refs[0], refs[1], refs[2 + len(after) :]
        out_ref, done, sems = refs
        stores = []
        rows = jnp.concatenate([ref[...] for ref in grads_refs])
        cols = jnp.concatenate([mine_ref[start:], sibling_ref[start:]])
        for k in range(parts):
            some = slice(k * step, (k + 1) * step)
            term = lax.dot_general(
                rows[:, some], cols, (((0,), (0,)), ((), ())), preferred_element_type=jnp.float32
            )
            done[some] = (partial_ref[some] + term).astype(done.dtype)
            stores.append(pltpu.make_async_copy(done.at[some], out_ref.at[some], sems.at[k]))
            stores[k].start()
        for store in stores:
            store.wait()

    ops = [partial, *grads, mine, sibling]
    return pl.pallas_call(
        body,
        out_shape=jax.ShapeDtypeStruct((vocab_rows, columns), jnp.bfloat16),
        in_specs=[WHOLE] * len(ops) + [ANY] * len(after),
        out_specs=ANY,
        scratch_shapes=[
            pltpu.VMEM(partial.shape, jnp.bfloat16),
            pltpu.SemaphoreType.DMA((parts,)),
        ],
        compiler_params=pltpu.CompilerParams(vmem_limit_bytes=16 * MIB),
        cost_estimate=cost(2 * count * vocab_rows * columns, ops),
    )(*ops, *after)


def shards(hidden, weight, teacher, block_ids):
    vocab_size = lax.axis_size("vocab")
    data_size = lax.axis_size("dp")
    rows, width = hidden.shape
    owned_blocks = weight.shape[0] // BLK
    chips = vocab_size // 2
    me = lax.axis_index("vocab")
    chip, core = place_on_mesh()

    pieces = [hidden]
    while 2 * len(pieces) < chips:
        pieces = pieces + [swap(piece, "vocab", 2 * len(pieces)) for piece in pieces]
    far = swap(hidden, "vocab", 2 * len(pieces))

    def between_chips(parts):
        return [parts[0]] + [swap(parts[r], "vocab", 2 * r) for r in range(1, chips)]

    def siblings_part(parts):
        given = [lax.dynamic_slice_in_dim(part, (1 - core) * rows, rows) for part in parts]
        return jnp.stack(given)

    pieces = pieces + [far] + [swap(far, "vocab", 2 * j) for j in range(1, len(pieces))]
    got = between_chips(
        [lax.dynamic_slice_in_dim(teacher, (chip ^ r) * 2 * rows, 2 * rows) for r in range(chips)]
    )
    own = jnp.concatenate(pieces)
    other = swap(own, "vocab", 1)
    my_ids = lax.dynamic_index_in_dim(block_ids, me * rows // BLK, keepdims=False)
    per = teacher.shape[1] // BLK
    owners = jnp.stack([(chip ^ r) * 2 + c for r in range(chips) for c in range(2)])
    blocks = (owners[:, None] * owned_blocks + jnp.arange(owned_blocks)[None, :]).reshape(-1)
    match = my_ids[None, :] == blocks[:, None]
    listed = jnp.any(match, axis=1).astype(jnp.int32)
    slots = jnp.argmax(match, axis=1).astype(jnp.int32)
    source = slots // per
    place = ((source % 2) ^ core) * chips + ((source // 2) ^ chip)
    placed = place_tiles(
        place * per + slots % per, listed, got, swap(siblings_part(got), "vocab", 1)
    )
    tiles = between_chips(placed)

    mass = jnp.sum(teacher, axis=1, dtype=jnp.float32)[None, :]

    logits, stats, kept, near, far = logits_and_stats(
        own, other, rows, weight, mass, width // data_size
    )
    own_cols = [swap_by_core(near), swap(far, "dp", data_size - 1)]

    stats = merge_pair(stats, swap(stats, "vocab", 1))
    all_stats = between_chips([stats] * chips)
    other_tiles = swap(siblings_part_after(tiles, rows, [stats]), "vocab", 1)
    spare = other_tiles[0, :TILE_ROWS, :BLK]
    grad_logits, share, rest, own_cols = logit_grads(
        logits, all_stats, tiles, other_tiles, weight, own_cols, [spare]
    )
    other_cols = swap(own_cols, "vocab", 1)

    share = share + swap(rest, "vocab", 1).astype(jnp.float32)
    shares = [share[j * rows : (j + 1) * rows] for j in range(chips)]
    count = 1
    while count < chips:
        for base in range(chips - 2 * count, -1, -2 * count):
            sent = swap(shares[base + count].astype(jnp.bfloat16), "vocab", 2 * count)
            shares[base] = shares[base] + sent.astype(jnp.float32)
        count *= 2
    grad_hidden = shares[0].astype(jnp.bfloat16)

    middle = grad_logits.shape[0] // 2
    near, far = swap(grad_logits, "dp", 1), swap(grad_logits, "dp", 2)
    last = [swap(near[:middle], "dp", 2), swap(far[middle:], "dp", 1)]
    partial = weight_grad_part([grad_logits, near, far], kept, own_cols, other_cols)
    grad_weight = weight_grad_rest(partial, last, own_cols, other_cols, [grad_hidden])
    return (grad_hidden, grad_weight)


def solution(mesh):
    placed = (P(("dp", "vocab"), None), P("vocab", None), P("dp", "vocab"), P("dp", None))

    def run(hidden, weight, teacher, block_ids):
        rows = hidden.shape[0] // (mesh.shape["dp"] * mesh.shape["vocab"])
        count = mesh.shape["vocab"]
        fits = count & (count - 1) == 0 and count > 2 and mesh.shape["dp"] == CORES**2
        fits = fits and rows % TILE_ROWS == 0 and BLK % rows == 0 and count * rows % (2 * BLK) == 0
        form = shards if fits else plain_shards
        return jax.shard_map(
            form,
            mesh=mesh,
            in_specs=placed,
            out_specs=(P(("dp", "vocab"), None), P("vocab", "dp")),
            check_vma=False,
        )(hidden, weight, teacher, block_ids)

    return run
```

```python
import jax
import jax.numpy as jnp
from jax import lax
from jax.experimental import pallas as pl
from jax.experimental.pallas import tpu as pltpu
from jax.sharding import PartitionSpec as P

BLK = 128
TILE_ROWS = 16
CORES = 2


loss_scale = 1024.0


def plain_shards(hidden, weight, teacher, block_ids):
    vocab_rows = weight.shape[0]
    owned_blocks = vocab_rows // BLK
    vocab_pos = lax.axis_index("vocab")
    full_hidden = lax.all_gather(hidden, "vocab", axis=0, tiled=True)
    token_count = full_hidden.shape[0]
    width = full_hidden.shape[1]
    logits = lax.dot_general(
        full_hidden, weight, (((1,), (1,)), ((), ())), preferred_element_type=jnp.float32
    )
    row_top = lax.pmax(jnp.max(logits, axis=1), "vocab")
    exp_terms = jnp.exp(logits - row_top[:, None])
    row_total = lax.psum(jnp.sum(exp_terms, axis=1), "vocab")
    block_count = token_count // BLK
    first_block = vocab_pos * owned_blocks
    block_range = jnp.arange(owned_blocks, dtype=jnp.int32)
    tile_cols = lax.all_gather(teacher, "vocab", axis=1, tiled=True)
    slot_count = tile_cols.shape[1] // BLK
    owned = block_ids - first_block
    onehot = (owned[:, :, None] == block_range[None, None, :]).astype(jnp.bfloat16)
    shaped = tile_cols.reshape(block_count, BLK, slot_count, BLK)
    target = jnp.einsum("bkv,btkc->btvc", onehot, shaped, preferred_element_type=jnp.float32)
    row_mass = jnp.sum(tile_cols, axis=1, dtype=jnp.float32)
    target = target.reshape(token_count, vocab_rows)
    grad_logits = (
        loss_scale * (row_mass[:, None] * (exp_terms / row_total[:, None]) - target)
    ).astype(jnp.bfloat16)
    grad_hidden = lax.psum_scatter(
        jnp.dot(grad_logits, weight, preferred_element_type=jnp.float32),
        "vocab",
        scatter_dimension=0,
        tiled=True,
    ).astype(jnp.bfloat16)
    data_count = lax.axis_size("dp")
    quarter = width // data_count
    split_hidden = full_hidden.reshape(token_count, data_count, quarter)
    quarter_rows = lax.all_to_all(
        split_hidden, "dp", split_axis=1, concat_axis=0, tiled=True
    ).reshape(token_count * data_count, quarter)
    grad_weight = lax.dot_general(
        lax.all_gather(grad_logits, "dp", axis=0, tiled=True),
        quarter_rows,
        (((0,), (0,)), ((), ())),
        preferred_element_type=jnp.float32,
    ).astype(jnp.bfloat16)
    return (grad_hidden, grad_weight)


def swap(x, axis, bits):
    return lax.ppermute(x, axis, [(i, i ^ bits) for i in range(lax.axis_size(axis))])


ANY = pl.BlockSpec(memory_space=pl.ANY)
WHOLE = pl.BlockSpec(memory_space=pltpu.VMEM)
SCALARS = pl.BlockSpec(memory_space=pltpu.SMEM)
MIB = 2**20


def in_hbm(x):
    return pltpu.with_memory_space_constraint(x, pltpu.HBM)


def place_on_mesh():
    me = lax.axis_index("vocab")
    return me // 2, lax.rem(me, 2)


def as_row(column):
    n = column.shape[0]
    same = lax.broadcasted_iota(jnp.int32, (n, n), 0) == lax.broadcasted_iota(jnp.int32, (n, n), 1)
    return jnp.sum(jnp.where(same, column, 0.0), axis=0, keepdims=True)


def as_column(row):
    n = row.shape[1]
    same = lax.broadcasted_iota(jnp.int32, (n, n), 0) == lax.broadcasted_iota(jnp.int32, (n, n), 1)
    return jnp.sum(jnp.where(same, row, 0.0), axis=1, keepdims=True)


def merge(stats):
    top = stats[0][0:1]
    for x in stats[1:]:
        top = jnp.maximum(top, x[0:1])
    total = sum(x[1:2] * jnp.exp(x[0:1] - top) for x in stats)
    mass = sum(x[2:3] for x in stats)
    return top, total, mass


def cost(flops, ops):
    return pl.CostEstimate(
        flops=flops, bytes_accessed=sum(op.size * 2 for op in ops), transcendentals=0
    )


def logits_and_stats(own, other, rows, weight, mass, quarter, parts=8, ahead=4):
    half, width = own.shape
    chips = half // rows
    tokens = 2 * half
    vocab_rows = weight.shape[0]
    step = vocab_rows // parts

    def body(*refs):
        piece_refs, refs = refs[:2], refs[2:]
        weight_ref, mass_ref, out_ref, stats_ref, refs = *refs[:4], refs[4:]
        kept_ref, near_ref, far_ref, held, held_weight, sems, piece_sems, cols_sems = refs
        chip, core = place_on_mesh()
        data_pos = lax.axis_index("dp")
        stores = []

        def store(h, group, target):
            column = pl.multiple_of(group * quarter, quarter)
            stores.append(
                pltpu.make_async_copy(
                    piece_refs[h].at[:, pl.ds(column, quarter)], target, cols_sems.at[len(stores)]
                )
            )
            stores[-1].start()

        loads = []
        for h in range(2):
            for j in range(chips):
                start = ((chip ^ j) * 2 + (core ^ h)) * rows
                n = h * chips + j
                loads.append(
                    pltpu.make_async_copy(
                        piece_refs[h].at[pl.ds(j * rows, rows)],
                        held.at[pl.ds(pl.multiple_of(start, rows), rows)],
                        piece_sems.at[n],
                    )
                )
                loads[n].start()
        copies = []
        for k in range(parts):
            some = pl.ds(k * step, step)
            copies.append(
                pltpu.make_async_copy(weight_ref.at[some], held_weight.at[some], sems.at[k])
            )
        for k in range(ahead):
            copies[k].start()
        for h in range(2):
            part = pl.ds(pl.multiple_of((core ^ h) * half, half), half)
            store(h, data_pos ^ (core + 1), near_ref.at[part])
            store(h, data_pos, kept_ref.at[part])
        store(0, data_pos ^ 3, far_ref)
        for load in loads:
            load.wait()
        for k in range(parts):
            copies[k].wait()
            if k + ahead < parts:
                copies[k + ahead].start()
            if (k + 1) % ahead == 0:
                some = slice((k + 1 - ahead) * step, (k + 1) * step)
                values = lax.dot_general(
                    held[...],
                    held_weight[some],
                    (((1,), (1,)), ((), ())),
                    preferred_element_type=jnp.float32,
                )
                out_ref[:, some] = values
                part_top = jnp.max(values, axis=1, keepdims=True)
                part_total = jnp.sum(jnp.exp(values - part_top), axis=1, keepdims=True)
                if k + 1 == ahead:
                    top, total = part_top, part_total
                else:
                    new_top = jnp.maximum(top, part_top)
                    total = total * jnp.exp(top - new_top)
                    total = total + part_total * jnp.exp(part_top - new_top)
                    top = new_top
        stats_ref[0:1] = as_row(top)
        stats_ref[1:2] = as_row(total)
        stats_ref[2:3] = mass_ref[...]
        stats_ref[3:8] = jnp.zeros((5, tokens), jnp.float32)
        for one in stores:
            one.wait()

    both = jax.ShapeDtypeStruct((tokens, quarter), own.dtype)
    ops = [own, other, in_hbm(weight), mass]
    return pl.pallas_call(
        body,
        out_shape=[
            jax.ShapeDtypeStruct((tokens, vocab_rows), jnp.float32),
            jax.ShapeDtypeStruct((8, tokens), jnp.float32),
            both,
            both,
            jax.ShapeDtypeStruct((half, quarter), own.dtype),
        ],
        in_specs=[ANY] * 3 + [WHOLE],
        out_specs=[WHOLE, WHOLE] + [ANY] * 3,
        scratch_shapes=[
            pltpu.VMEM((tokens, width), weight.dtype),
            pltpu.VMEM(weight.shape, weight.dtype),
            pltpu.SemaphoreType.DMA((parts,)),
            pltpu.SemaphoreType.DMA((2 * chips,)),
            pltpu.SemaphoreType.DMA((5,)),
        ],
        compiler_params=pltpu.CompilerParams(vmem_limit_bytes=32 * MIB),
        cost_estimate=cost(2 * tokens * weight.size, ops),
    )(*ops)


def swap_by_core(x):
    count = lax.axis_size("vocab")
    pairs = [
        (d * count + v, (d ^ (v % 2 + 1)) * count + v)
        for d in range(lax.axis_size("dp"))
        for v in range(count)
    ]
    return lax.ppermute(x, ("dp", "vocab"), pairs)


def merge_pair(a, b, after=()):
    def body(a_ref, b_ref, *refs):
        out_ref = refs[-1]
        for k, row in enumerate(merge([a_ref[...], b_ref[...]])):
            out_ref[k : k + 1] = row
        out_ref[3:8] = jnp.zeros((5, a.shape[1]), jnp.float32)

    return pl.pallas_call(
        body,
        out_shape=jax.ShapeDtypeStruct(a.shape, a.dtype),
        in_specs=[WHOLE, WHOLE] + [ANY] * len(after),
        out_specs=WHOLE,
        compiler_params=pltpu.CompilerParams(vmem_limit_bytes=MIB),
        cost_estimate=cost(0, (a, b)),
    )(a, b, *after)


def siblings_part_after(parts, rows, after):
    def body(*refs):
        start = pl.multiple_of((1 - place_on_mesh()[1]) * rows, rows)
        for j in range(len(parts)):
            refs[-1][j] = refs[j][pl.ds(start, rows), :]

    return pl.pallas_call(
        body,
        out_shape=jax.ShapeDtypeStruct((len(parts), rows, parts[0].shape[1]), parts[0].dtype),
        in_specs=[WHOLE] * len(parts) + [ANY] * len(after),
        out_specs=WHOLE,
        compiler_params=pltpu.CompilerParams(vmem_limit_bytes=4 * MIB),
        cost_estimate=cost(0, parts),
    )(*parts, *after)


def place_tiles(slots, listed, mine, sibling, after):
    chips, rows, columns = sibling.shape
    per = columns // BLK
    owned = slots.shape[0] // (2 * chips)

    def body(slots_ref, listed_ref, *refs):
        mine_refs, sibling_ref = refs[:chips], refs[chips]
        outs, held = refs[-chips - 1 : -1], refs[-1]
        start = pl.multiple_of(place_on_mesh()[1] * rows, rows)
        for j in range(chips):
            held[j] = mine_refs[j][pl.ds(start, rows), :]
            held[chips + j] = sibling_ref[j]
        for r in range(chips):
            for c in range(2):
                for v in range(owned):
                    n = (r * 2 + c) * owned + v
                    slot = slots_ref[n]
                    column = pl.multiple_of(lax.rem(slot, per) * BLK, BLK)
                    tile = held[slot // per, :, pl.ds(column, BLK)]
                    outs[r][c * rows : (c + 1) * rows, v * BLK : (v + 1) * BLK] = jnp.where(
                        listed_ref[n] > 0, tile, jnp.zeros_like(tile)
                    )

    shape = jax.ShapeDtypeStruct((2 * rows, owned * BLK), sibling.dtype)
    return pl.pallas_call(
        body,
        out_shape=[shape] * chips,
        in_specs=[SCALARS] * 2 + [WHOLE] * (chips + 1) + [ANY] * len(after),
        out_specs=[WHOLE] * chips,
        scratch_shapes=[pltpu.VMEM((2 * chips, rows, columns), sibling.dtype)],
        compiler_params=pltpu.CompilerParams(vmem_limit_bytes=16 * MIB),
        cost_estimate=cost(0, (sibling, sibling)),
    )(slots, listed, *mine, sibling, *after)


def logit_grads(logits, stats, mine, sibling, weight, cols, after, parts=4, ahead=3):
    chips, rows, vocab_rows = sibling.shape
    tokens = logits.shape[0]
    half = chips * rows
    width = weight.shape[1]
    step = width // parts
    count = len(stats)

    def body(logits_ref, *refs):
        stats_refs, refs = refs[:count], refs[count:]
        mine_refs, refs = refs[:chips], refs[chips:]
        sibling_ref, weight_ref, refs = refs[0], refs[1], refs[2:]
        cols_refs, refs = refs[: len(cols)], refs[len(cols) + len(after) :]
        out_ref, own_ref, other_ref, stacked_ref, held_weight, columns, sems, cols_sems = refs
        moves = []
        for r, ref in enumerate(cols_refs):
            at = sum(x.shape[0] for x in cols[:r])
            target = stacked_ref.at[at : at + cols[r].shape[0]]
            moves.append(pltpu.make_async_copy(ref, target, cols_sems.at[r]))
        copies = []
        for k in range(parts):
            some = pl.ds(k * step, step)
            copies.append(
                pltpu.make_async_copy(
                    weight_ref.at[:, some], held_weight.at[:, some], sems.at[k]
                )
            )
        for k in range(ahead):
            copies[k].start()
        for move in moves:
            move.start()
        top, total, mass = merge([ref[...] for ref in stats_refs])
        columns[:, 0:1] = as_column(top)
        columns[:, 1:2] = as_column(loss_scale * mass / total)
        chip, core = place_on_mesh()
        mine_start = pl.multiple_of(core * rows, rows)
        for h in range(2):
            for j in range(chips):
                start = ((chip ^ j) * 2 + (core ^ h)) * rows
                part = pl.ds(pl.multiple_of(start, rows), rows)
                tiles = sibling_ref[j] if h else mine_refs[j][pl.ds(mine_start, rows), :]
                grads = (
                    columns[part, 1:2] * jnp.exp(logits_ref[part, :] - columns[part, 0:1])
                    - loss_scale * tiles.astype(jnp.float32)
                ).astype(out_ref.dtype)
                out_ref[(h * chips + j) * rows : (h * chips + j + 1) * rows] = grads
        for k in range(parts):
            copies[k].wait()
            if k + ahead < parts:
                copies[k + ahead].start()
            some = slice(k * step, (k + 1) * step)
            share = jnp.dot(out_ref[...], held_weight[:, some], preferred_element_type=jnp.float32)
            own_ref[:, some] = share[:half]
            other_ref[:, some] = share[half:].astype(other_ref.dtype)
        for move in moves:
            move.wait()

    ops = (logits, *stats, *mine, sibling, in_hbm(weight))
    return pl.pallas_call(
        body,
        out_shape=[
            jax.ShapeDtypeStruct((tokens, vocab_rows), jnp.bfloat16),
            jax.ShapeDtypeStruct((half, width), jnp.float32),
            jax.ShapeDtypeStruct((half, width), jnp.bfloat16),
            jax.ShapeDtypeStruct((sum(x.shape[0] for x in cols), cols[0].shape[1]), cols[0].dtype),
        ],
        in_specs=[WHOLE] * (len(ops) - 1) + [ANY] * (1 + len(cols) + len(after)),
        out_specs=[WHOLE] * 3 + [ANY],
        scratch_shapes=[
            pltpu.VMEM(weight.shape, weight.dtype),
            pltpu.VMEM((tokens, 128), jnp.float32),
            pltpu.SemaphoreType.DMA((parts,)),
            pltpu.SemaphoreType.DMA((len(cols),)),
        ],
        compiler_params=pltpu.CompilerParams(vmem_limit_bytes=32 * MIB),
        cost_estimate=cost(2 * weight.size * tokens, ops),
    )(*ops, *cols, *after)


def ordered_columns(kept, mine, sibling):
    tokens = kept.shape[0]
    half = tokens // 2
    first = place_on_mesh()[1] == 0
    a, b = mine[:tokens], sibling[:tokens]
    cols = []
    for group in (kept[...], jnp.where(first, a, b), jnp.where(first, b, a)):
        low, high = group[:half], group[half:]
        cols += [jnp.where(first, low, high), jnp.where(first, high, low)]
    return jnp.concatenate(cols)


def weight_grad_part(grads, kept, mine, sibling):
    vocab_rows = grads[0].shape[1]
    tokens, columns = kept.shape

    def body(*refs):
        kept_ref, mine_ref, sibling_ref, out_ref = refs[len(grads) :]
        out_ref[...] = lax.dot_general(
            jnp.concatenate([ref[...] for ref in refs[: len(grads)]]),
            ordered_columns(kept_ref, mine_ref, sibling_ref),
            (((0,), (0,)), ((), ())),
            preferred_element_type=jnp.float32,
        )

    ops = [*grads, kept, mine, sibling]
    return pl.pallas_call(
        body,
        out_shape=jax.ShapeDtypeStruct((vocab_rows, columns), jnp.float32),
        in_specs=[WHOLE] * len(ops),
        out_specs=WHOLE,
        compiler_params=pltpu.CompilerParams(vmem_limit_bytes=24 * MIB),
        cost_estimate=cost(6 * tokens * vocab_rows * columns, ops),
    )(*ops)


def weight_grad_rest(partial, grads, mine, sibling, after, parts=4):
    vocab_rows, columns = partial.shape
    step = vocab_rows // parts
    count = sum(x.shape[0] for x in grads)
    start = mine.shape[0] - count // 2

    def body(partial_ref, *refs):
        grads_refs, refs = refs[: len(grads)], refs[len(grads) :]
        mine_ref, sibling_ref, refs = refs[0], refs[1], refs[2 + len(after) :]
        out_ref, done, sems = refs
        stores = []
        rows = jnp.concatenate([ref[...] for ref in grads_refs])
        cols = jnp.concatenate([mine_ref[start:], sibling_ref[start:]])
        for k in range(parts):
            some = slice(k * step, (k + 1) * step)
            term = lax.dot_general(
                rows[:, some], cols, (((0,), (0,)), ((), ())), preferred_element_type=jnp.float32
            )
            done[some] = (partial_ref[some] + term).astype(done.dtype)
            stores.append(pltpu.make_async_copy(done.at[some], out_ref.at[some], sems.at[k]))
            stores[k].start()
        for store in stores:
            store.wait()

    ops = [partial, *grads, mine, sibling]
    return pl.pallas_call(
        body,
        out_shape=jax.ShapeDtypeStruct((vocab_rows, columns), jnp.bfloat16),
        in_specs=[WHOLE] * len(ops) + [ANY] * len(after),
        out_specs=ANY,
        scratch_shapes=[
            pltpu.VMEM(partial.shape, jnp.bfloat16),
            pltpu.SemaphoreType.DMA((parts,)),
        ],
        compiler_params=pltpu.CompilerParams(vmem_limit_bytes=16 * MIB),
        cost_estimate=cost(2 * count * vocab_rows * columns, ops),
    )(*ops, *after)


def shards(hidden, weight, teacher, block_ids):
    vocab_size = lax.axis_size("vocab")
    data_size = lax.axis_size("dp")
    rows, width = hidden.shape
    owned_blocks = weight.shape[0] // BLK
    chips = vocab_size // 2
    me = lax.axis_index("vocab")
    chip, core = place_on_mesh()

    pieces = [hidden]
    while 2 * len(pieces) < chips:
        pieces = pieces + [swap(piece, "vocab", 2 * len(pieces)) for piece in pieces]
    far = swap(hidden, "vocab", 2 * len(pieces))

    def between_chips(parts):
        return [parts[0]] + [swap(parts[r], "vocab", 2 * r) for r in range(1, chips)]

    def siblings_part(parts):
        given = [lax.dynamic_slice_in_dim(part, (1 - core) * rows, rows) for part in parts]
        return jnp.stack(given)

    halves = [
        [swap(far[k : k + rows // 2], "vocab", 2 * j) for k in (0, rows // 2)]
        for j in range(1, len(pieces))
    ]
    got = between_chips(
        [lax.dynamic_slice_in_dim(teacher, (chip ^ r) * 2 * rows, 2 * rows) for r in range(chips)]
    )
    firsts, got = lax.optimization_barrier(([pair[0] for pair in halves], got))
    seconds = [pair[1] for pair in halves]
    pieces = pieces + [far] + [part for pair in zip(firsts, seconds) for part in pair]
    own = jnp.concatenate(pieces)
    other = swap(own, "vocab", 1)
    my_ids = lax.dynamic_index_in_dim(block_ids, me * rows // BLK, keepdims=False)
    per = teacher.shape[1] // BLK
    owners = jnp.stack([(chip ^ r) * 2 + c for r in range(chips) for c in range(2)])
    blocks = (owners[:, None] * owned_blocks + jnp.arange(owned_blocks)[None, :]).reshape(-1)
    match = my_ids[None, :] == blocks[:, None]
    listed = jnp.any(match, axis=1).astype(jnp.int32)
    slots = jnp.argmax(match, axis=1).astype(jnp.int32)
    source = slots // per
    place = ((source % 2) ^ core) * chips + ((source // 2) ^ chip)
    from_sibling = swap(siblings_part(got), "vocab", 1)
    seen = from_sibling[0, :TILE_ROWS, :BLK]
    seen = lax.optimization_barrier(seen) * jnp.bfloat16(0.5)
    placed = place_tiles(place * per + slots % per, listed, got, from_sibling, [seen])
    tiles = between_chips(placed)

    mass = jnp.sum(teacher, axis=1, dtype=jnp.float32)[None, :]

    logits, stats, kept, near, far = logits_and_stats(
        own, other, rows, weight, mass, width // data_size
    )
    own_cols = [swap_by_core(near), swap(far, "dp", data_size - 1)]

    stats = merge_pair(stats, swap(stats, "vocab", 1))
    all_stats = between_chips([stats] * chips)
    other_tiles = swap(siblings_part_after(tiles, rows, [stats]), "vocab", 1)
    spare = other_tiles[0, :TILE_ROWS, :BLK]
    grad_logits, share, rest, own_cols = logit_grads(
        logits, all_stats, tiles, other_tiles, weight, own_cols, [spare]
    )
    other_cols = swap(own_cols, "vocab", 1)

    share = share + swap(rest, "vocab", 1).astype(jnp.float32)
    shares = [share[j * rows : (j + 1) * rows] for j in range(chips)]
    count = 1
    while count < chips:
        for base in range(chips - 2 * count, -1, -2 * count):
            sent = swap(shares[base + count].astype(jnp.bfloat16), "vocab", 2 * count)
            shares[base] = shares[base] + sent.astype(jnp.float32)
        count *= 2
    grad_hidden = shares[0].astype(jnp.bfloat16)

    middle = grad_logits.shape[0] // 2
    near, far = swap(grad_logits, "dp", 1), swap(grad_logits, "dp", 2)
    last = [swap(near[:middle], "dp", 2), swap(far[middle:], "dp", 1)]
    partial = weight_grad_part([grad_logits, near, far], kept, own_cols, other_cols)
    grad_weight = weight_grad_rest(partial, last, own_cols, other_cols, [grad_hidden])
    return (grad_hidden, grad_weight)


def solution(mesh):
    placed = (P(("dp", "vocab"), None), P("vocab", None), P("dp", "vocab"), P("dp", None))

    def run(hidden, weight, teacher, block_ids):
        rows = hidden.shape[0] // (mesh.shape["dp"] * mesh.shape["vocab"])
        count = mesh.shape["vocab"]
        fits = count & (count - 1) == 0 and count > 2 and mesh.shape["dp"] == CORES**2
        fits = fits and rows % TILE_ROWS == 0 and BLK % rows == 0 and count * rows % (2 * BLK) == 0
        form = shards if fits else plain_shards
        return jax.shard_map(
            form,
            mesh=mesh,
            in_specs=placed,
            out_specs=(P(("dp", "vocab"), None), P("vocab", "dp")),
            check_vma=False,
        )(hidden, weight, teacher, block_ids)

    return run
```

```python
import jax
import jax.numpy as jnp
from jax import lax
from jax.experimental import pallas as pl
from jax.experimental.pallas import tpu as pltpu
from jax.sharding import PartitionSpec as P

BLK = 128
TILE_ROWS = 16
CORES = 2


loss_scale = 1024.0


def plain_shards(hidden, weight, teacher, block_ids):
    vocab_rows = weight.shape[0]
    owned_blocks = vocab_rows // BLK
    vocab_pos = lax.axis_index("vocab")
    full_hidden = lax.all_gather(hidden, "vocab", axis=0, tiled=True)
    token_count = full_hidden.shape[0]
    width = full_hidden.shape[1]
    logits = lax.dot_general(
        full_hidden, weight, (((1,), (1,)), ((), ())), preferred_element_type=jnp.float32
    )
    row_top = lax.pmax(jnp.max(logits, axis=1), "vocab")
    exp_terms = jnp.exp(logits - row_top[:, None])
    row_total = lax.psum(jnp.sum(exp_terms, axis=1), "vocab")
    block_count = token_count // BLK
    first_block = vocab_pos * owned_blocks
    block_range = jnp.arange(owned_blocks, dtype=jnp.int32)
    tile_cols = lax.all_gather(teacher, "vocab", axis=1, tiled=True)
    slot_count = tile_cols.shape[1] // BLK
    owned = block_ids - first_block
    onehot = (owned[:, :, None] == block_range[None, None, :]).astype(jnp.bfloat16)
    shaped = tile_cols.reshape(block_count, BLK, slot_count, BLK)
    target = jnp.einsum("bkv,btkc->btvc", onehot, shaped, preferred_element_type=jnp.float32)
    row_mass = jnp.sum(tile_cols, axis=1, dtype=jnp.float32)
    target = target.reshape(token_count, vocab_rows)
    grad_logits = (
        loss_scale * (row_mass[:, None] * (exp_terms / row_total[:, None]) - target)
    ).astype(jnp.bfloat16)
    grad_hidden = lax.psum_scatter(
        jnp.dot(grad_logits, weight, preferred_element_type=jnp.float32),
        "vocab",
        scatter_dimension=0,
        tiled=True,
    ).astype(jnp.bfloat16)
    data_count = lax.axis_size("dp")
    quarter = width // data_count
    split_hidden = full_hidden.reshape(token_count, data_count, quarter)
    quarter_rows = lax.all_to_all(
        split_hidden, "dp", split_axis=1, concat_axis=0, tiled=True
    ).reshape(token_count * data_count, quarter)
    grad_weight = lax.dot_general(
        lax.all_gather(grad_logits, "dp", axis=0, tiled=True),
        quarter_rows,
        (((0,), (0,)), ((), ())),
        preferred_element_type=jnp.float32,
    ).astype(jnp.bfloat16)
    return (grad_hidden, grad_weight)


def swap(x, axis, bits):
    return lax.ppermute(x, axis, [(i, i ^ bits) for i in range(lax.axis_size(axis))])


ANY = pl.BlockSpec(memory_space=pl.ANY)
WHOLE = pl.BlockSpec(memory_space=pltpu.VMEM)
SCALARS = pl.BlockSpec(memory_space=pltpu.SMEM)
MIB = 2**20


def in_hbm(x):
    return pltpu.with_memory_space_constraint(x, pltpu.HBM)


def place_on_mesh():
    me = lax.axis_index("vocab")
    return me // 2, lax.rem(me, 2)


def as_row(column):
    n = column.shape[0]
    same = lax.broadcasted_iota(jnp.int32, (n, n), 0) == lax.broadcasted_iota(jnp.int32, (n, n), 1)
    return jnp.sum(jnp.where(same, column, 0.0), axis=0, keepdims=True)


def as_column(row):
    n = row.shape[1]
    same = lax.broadcasted_iota(jnp.int32, (n, n), 0) == lax.broadcasted_iota(jnp.int32, (n, n), 1)
    return jnp.sum(jnp.where(same, row, 0.0), axis=1, keepdims=True)


def merge(stats):
    top = stats[0][0:1]
    for x in stats[1:]:
        top = jnp.maximum(top, x[0:1])
    total = sum(x[1:2] * jnp.exp(x[0:1] - top) for x in stats)
    mass = sum(x[2:3] for x in stats)
    return top, total, mass


def cost(flops, ops):
    return pl.CostEstimate(
        flops=flops, bytes_accessed=sum(op.size * 2 for op in ops), transcendentals=0
    )


def logits_and_stats(own, other, rows, weight, mass, quarter, parts=8, ahead=4):
    half, width = own.shape
    chips = half // rows
    tokens = 2 * half
    vocab_rows = weight.shape[0]
    step = vocab_rows // parts

    def body(*refs):
        piece_refs, refs = refs[:2], refs[2:]
        weight_ref, mass_ref, out_ref, stats_ref, refs = *refs[:4], refs[4:]
        kept_ref, near_ref, far_ref, held, held_weight, sems, piece_sems, cols_sems = refs
        chip, core = place_on_mesh()
        data_pos = lax.axis_index("dp")
        stores = []

        def store(h, group, target):
            column = pl.multiple_of(group * quarter, quarter)
            stores.append(
                pltpu.make_async_copy(
                    piece_refs[h].at[:, pl.ds(column, quarter)], target, cols_sems.at[len(stores)]
                )
            )
            stores[-1].start()

        loads = []
        for h in range(2):
            for j in range(chips):
                start = ((chip ^ j) * 2 + (core ^ h)) * rows
                n = h * chips + j
                loads.append(
                    pltpu.make_async_copy(
                        piece_refs[h].at[pl.ds(j * rows, rows)],
                        held.at[pl.ds(pl.multiple_of(start, rows), rows)],
                        piece_sems.at[n],
                    )
                )
                loads[n].start()
        copies = []
        for k in range(parts):
            some = pl.ds(k * step, step)
            copies.append(
                pltpu.make_async_copy(weight_ref.at[some], held_weight.at[some], sems.at[k])
            )
        for k in range(ahead):
            copies[k].start()
        for h in range(2):
            part = pl.ds(pl.multiple_of((core ^ h) * half, half), half)
            store(h, data_pos ^ (core + 1), near_ref.at[part])
            store(h, data_pos, kept_ref.at[part])
        store(0, data_pos ^ 3, far_ref)
        for load in loads:
            load.wait()
        for k in range(parts):
            copies[k].wait()
            if k + ahead < parts:
                copies[k + ahead].start()
            if (k + 1) % ahead == 0:
                some = slice((k + 1 - ahead) * step, (k + 1) * step)
                values = lax.dot_general(
                    held[...],
                    held_weight[some],
                    (((1,), (1,)), ((), ())),
                    preferred_element_type=jnp.float32,
                )
                out_ref[:, some] = values
                part_top = jnp.max(values, axis=1, keepdims=True)
                part_total = jnp.sum(jnp.exp(values - part_top), axis=1, keepdims=True)
                if k + 1 == ahead:
                    top, total = part_top, part_total
                else:
                    new_top = jnp.maximum(top, part_top)
                    total = total * jnp.exp(top - new_top)
                    total = total + part_total * jnp.exp(part_top - new_top)
                    top = new_top
        stats_ref[0:1] = as_row(top)
        stats_ref[1:2] = as_row(total)
        stats_ref[2:3] = mass_ref[...]
        stats_ref[3:8] = jnp.zeros((5, tokens), jnp.float32)
        for one in stores:
            one.wait()

    both = jax.ShapeDtypeStruct((tokens, quarter), own.dtype)
    ops = [own, other, in_hbm(weight), mass]
    return pl.pallas_call(
        body,
        out_shape=[
            jax.ShapeDtypeStruct((tokens, vocab_rows), jnp.float32),
            jax.ShapeDtypeStruct((8, tokens), jnp.float32),
            both,
            both,
            jax.ShapeDtypeStruct((half, quarter), own.dtype),
        ],
        in_specs=[ANY] * 3 + [WHOLE],
        out_specs=[WHOLE, WHOLE] + [ANY] * 3,
        scratch_shapes=[
            pltpu.VMEM((tokens, width), weight.dtype),
            pltpu.VMEM(weight.shape, weight.dtype),
            pltpu.SemaphoreType.DMA((parts,)),
            pltpu.SemaphoreType.DMA((2 * chips,)),
            pltpu.SemaphoreType.DMA((5,)),
        ],
        compiler_params=pltpu.CompilerParams(vmem_limit_bytes=32 * MIB),
        cost_estimate=cost(2 * tokens * weight.size, ops),
    )(*ops)


def swap_by_core(x):
    count = lax.axis_size("vocab")
    pairs = [
        (d * count + v, (d ^ (v % 2 + 1)) * count + v)
        for d in range(lax.axis_size("dp"))
        for v in range(count)
    ]
    return lax.ppermute(x, ("dp", "vocab"), pairs)


def merge_pair(a, b, after=()):
    def body(a_ref, b_ref, *refs):
        out_ref = refs[-1]
        for k, row in enumerate(merge([a_ref[...], b_ref[...]])):
            out_ref[k : k + 1] = row
        out_ref[3:8] = jnp.zeros((5, a.shape[1]), jnp.float32)

    return pl.pallas_call(
        body,
        out_shape=jax.ShapeDtypeStruct(a.shape, a.dtype),
        in_specs=[WHOLE, WHOLE] + [ANY] * len(after),
        out_specs=WHOLE,
        compiler_params=pltpu.CompilerParams(vmem_limit_bytes=MIB),
        cost_estimate=cost(0, (a, b)),
    )(a, b, *after)


def siblings_part_after(parts, rows, after):
    def body(*refs):
        start = pl.multiple_of((1 - place_on_mesh()[1]) * rows, rows)
        for j in range(len(parts)):
            refs[-1][j] = refs[j][pl.ds(start, rows), :]

    return pl.pallas_call(
        body,
        out_shape=jax.ShapeDtypeStruct((len(parts), rows, parts[0].shape[1]), parts[0].dtype),
        in_specs=[WHOLE] * len(parts) + [ANY] * len(after),
        out_specs=WHOLE,
        compiler_params=pltpu.CompilerParams(vmem_limit_bytes=4 * MIB),
        cost_estimate=cost(0, parts),
    )(*parts, *after)


def place_tiles(slots, listed, mine, sibling, after):
    chips, rows, columns = sibling.shape
    per = columns // BLK
    owned = slots.shape[0] // (2 * chips)

    def body(slots_ref, listed_ref, *refs):
        mine_refs, sibling_ref = refs[:chips], refs[chips]
        outs, held = refs[-chips - 1 : -1], refs[-1]
        start = pl.multiple_of(place_on_mesh()[1] * rows, rows)
        for j in range(chips):
            held[j] = mine_refs[j][pl.ds(start, rows), :]
            held[chips + j] = sibling_ref[j]
        for r in range(chips):
            for c in range(2):
                for v in range(owned):
                    n = (r * 2 + c) * owned + v
                    slot = slots_ref[n]
                    column = pl.multiple_of(lax.rem(slot, per) * BLK, BLK)
                    tile = held[slot // per, :, pl.ds(column, BLK)]
                    outs[r][c * rows : (c + 1) * rows, v * BLK : (v + 1) * BLK] = jnp.where(
                        listed_ref[n] > 0, tile, jnp.zeros_like(tile)
                    )

    shape = jax.ShapeDtypeStruct((2 * rows, owned * BLK), sibling.dtype)
    return pl.pallas_call(
        body,
        out_shape=[shape] * chips,
        in_specs=[SCALARS] * 2 + [WHOLE] * (chips + 1) + [ANY] * len(after),
        out_specs=[WHOLE] * chips,
        scratch_shapes=[pltpu.VMEM((2 * chips, rows, columns), sibling.dtype)],
        compiler_params=pltpu.CompilerParams(vmem_limit_bytes=16 * MIB),
        cost_estimate=cost(0, (sibling, sibling)),
    )(slots, listed, *mine, sibling, *after)


def logit_grads(logits, stats, mine, sibling, weight, cols, after, parts=4, ahead=3):
    chips, rows, vocab_rows = sibling.shape
    tokens = logits.shape[0]
    half = chips * rows
    width = weight.shape[1]
    step = width // parts
    count = len(stats)

    def body(logits_ref, *refs):
        stats_refs, refs = refs[:count], refs[count:]
        mine_refs, refs = refs[:chips], refs[chips:]
        sibling_ref, weight_ref, refs = refs[0], refs[1], refs[2:]
        cols_refs, refs = refs[: len(cols)], refs[len(cols) + len(after) :]
        out_ref, own_ref, other_ref, stacked_ref, held_weight, columns, sems, cols_sems = refs
        moves = []
        for r, ref in enumerate(cols_refs):
            at = sum(x.shape[0] for x in cols[:r])
            target = stacked_ref.at[at : at + cols[r].shape[0]]
            moves.append(pltpu.make_async_copy(ref, target, cols_sems.at[r]))
        copies = []
        for k in range(parts):
            some = pl.ds(k * step, step)
            copies.append(
                pltpu.make_async_copy(
                    weight_ref.at[:, some], held_weight.at[:, some], sems.at[k]
                )
            )
        for k in range(ahead):
            copies[k].start()
        for move in moves:
            move.start()
        top, total, mass = merge([ref[...] for ref in stats_refs])
        columns[:, 0:1] = as_column(top)
        columns[:, 1:2] = as_column(loss_scale * mass / total)
        chip, core = place_on_mesh()
        mine_start = pl.multiple_of(core * rows, rows)
        for h in range(2):
            for j in range(chips):
                start = ((chip ^ j) * 2 + (core ^ h)) * rows
                part = pl.ds(pl.multiple_of(start, rows), rows)
                tiles = sibling_ref[j] if h else mine_refs[j][pl.ds(mine_start, rows), :]
                grads = (
                    columns[part, 1:2] * jnp.exp(logits_ref[part, :] - columns[part, 0:1])
                    - loss_scale * tiles.astype(jnp.float32)
                ).astype(out_ref.dtype)
                out_ref[(h * chips + j) * rows : (h * chips + j + 1) * rows] = grads
        for k in range(parts):
            copies[k].wait()
            if k + ahead < parts:
                copies[k + ahead].start()
            some = slice(k * step, (k + 1) * step)
            share = jnp.dot(out_ref[...], held_weight[:, some], preferred_element_type=jnp.float32)
            own_ref[:, some] = share[:half]
            other_ref[:, some] = share[half:].astype(other_ref.dtype)
        for move in moves:
            move.wait()

    ops = (logits, *stats, *mine, sibling, in_hbm(weight))
    return pl.pallas_call(
        body,
        out_shape=[
            jax.ShapeDtypeStruct((tokens, vocab_rows), jnp.bfloat16),
            jax.ShapeDtypeStruct((half, width), jnp.float32),
            jax.ShapeDtypeStruct((half, width), jnp.bfloat16),
            jax.ShapeDtypeStruct((sum(x.shape[0] for x in cols), cols[0].shape[1]), cols[0].dtype),
        ],
        in_specs=[WHOLE] * (len(ops) - 1) + [ANY] * (1 + len(cols) + len(after)),
        out_specs=[WHOLE] * 3 + [ANY],
        scratch_shapes=[
            pltpu.VMEM(weight.shape, weight.dtype),
            pltpu.VMEM((tokens, 128), jnp.float32),
            pltpu.SemaphoreType.DMA((parts,)),
            pltpu.SemaphoreType.DMA((len(cols),)),
        ],
        compiler_params=pltpu.CompilerParams(vmem_limit_bytes=32 * MIB),
        cost_estimate=cost(2 * weight.size * tokens, ops),
    )(*ops, *cols, *after)


def ordered_columns(kept, mine, sibling):
    tokens = kept.shape[0]
    half = tokens // 2
    first = place_on_mesh()[1] == 0
    a, b = mine[:tokens], sibling[:tokens]
    cols = []
    for group in (kept[...], jnp.where(first, a, b), jnp.where(first, b, a)):
        low, high = group[:half], group[half:]
        cols += [jnp.where(first, low, high), jnp.where(first, high, low)]
    return jnp.concatenate(cols)


def weight_grad_part(grads, kept, mine, sibling):
    vocab_rows = grads[0].shape[1]
    tokens, columns = kept.shape

    def body(*refs):
        kept_ref, mine_ref, sibling_ref, out_ref = refs[len(grads) :]
        out_ref[...] = lax.dot_general(
            jnp.concatenate([ref[...] for ref in refs[: len(grads)]]),
            ordered_columns(kept_ref, mine_ref, sibling_ref),
            (((0,), (0,)), ((), ())),
            preferred_element_type=jnp.float32,
        )

    ops = [*grads, kept, mine, sibling]
    return pl.pallas_call(
        body,
        out_shape=jax.ShapeDtypeStruct((vocab_rows, columns), jnp.float32),
        in_specs=[WHOLE] * len(ops),
        out_specs=WHOLE,
        compiler_params=pltpu.CompilerParams(vmem_limit_bytes=24 * MIB),
        cost_estimate=cost(6 * tokens * vocab_rows * columns, ops),
    )(*ops)


def weight_grad_rest(partial, grads, mine, sibling, after, parts=4):
    vocab_rows, columns = partial.shape
    step = vocab_rows // parts
    count = sum(x.shape[0] for x in grads)
    start = mine.shape[0] - count // 2

    def body(partial_ref, *refs):
        grads_refs, refs = refs[: len(grads)], refs[len(grads) :]
        mine_ref, sibling_ref, refs = refs[0], refs[1], refs[2 + len(after) :]
        out_ref, done, sems = refs
        stores = []
        rows = jnp.concatenate([ref[...] for ref in grads_refs])
        cols = jnp.concatenate([mine_ref[start:], sibling_ref[start:]])
        for k in range(parts):
            some = slice(k * step, (k + 1) * step)
            term = lax.dot_general(
                rows[:, some], cols, (((0,), (0,)), ((), ())), preferred_element_type=jnp.float32
            )
            done[some] = (partial_ref[some] + term).astype(done.dtype)
            stores.append(pltpu.make_async_copy(done.at[some], out_ref.at[some], sems.at[k]))
            stores[k].start()
        for store in stores:
            store.wait()

    ops = [partial, *grads, mine, sibling]
    return pl.pallas_call(
        body,
        out_shape=jax.ShapeDtypeStruct((vocab_rows, columns), jnp.bfloat16),
        in_specs=[WHOLE] * len(ops) + [ANY] * len(after),
        out_specs=ANY,
        scratch_shapes=[
            pltpu.VMEM(partial.shape, jnp.bfloat16),
            pltpu.SemaphoreType.DMA((parts,)),
        ],
        compiler_params=pltpu.CompilerParams(vmem_limit_bytes=16 * MIB),
        cost_estimate=cost(2 * count * vocab_rows * columns, ops),
    )(*ops, *after)


def shards(hidden, weight, teacher, block_ids):
    vocab_size = lax.axis_size("vocab")
    data_size = lax.axis_size("dp")
    rows, width = hidden.shape
    owned_blocks = weight.shape[0] // BLK
    chips = vocab_size // 2
    me = lax.axis_index("vocab")
    chip, core = place_on_mesh()

    pieces = [hidden]
    while 2 * len(pieces) < chips:
        pieces = pieces + [swap(piece, "vocab", 2 * len(pieces)) for piece in pieces]
    far = swap(hidden, "vocab", 2 * len(pieces))

    def between_chips(parts):
        moved = [swap(parts[r], "vocab", 2 * r) for r in reversed(range(1, chips))]
        return [parts[0]] + moved[::-1]

    def siblings_part(parts):
        given = [lax.dynamic_slice_in_dim(part, (1 - core) * rows, rows) for part in parts]
        return jnp.stack(given)

    halves = [
        [swap(far[k : k + rows // 2], "vocab", 2 * j) for k in (0, rows // 2)]
        for j in range(1, len(pieces))
    ]
    got = between_chips(
        [lax.dynamic_slice_in_dim(teacher, (chip ^ r) * 2 * rows, 2 * rows) for r in range(chips)]
    )
    firsts, got = lax.optimization_barrier(([pair[0] for pair in halves], got))
    seconds = [pair[1] for pair in halves]
    pieces = pieces + [far] + [part for pair in zip(firsts, seconds) for part in pair]
    own = jnp.concatenate(pieces)
    other = swap(own, "vocab", 1)
    my_ids = lax.dynamic_index_in_dim(block_ids, me * rows // BLK, keepdims=False)
    per = teacher.shape[1] // BLK
    owners = jnp.stack([(chip ^ r) * 2 + c for r in range(chips) for c in range(2)])
    blocks = (owners[:, None] * owned_blocks + jnp.arange(owned_blocks)[None, :]).reshape(-1)
    match = my_ids[None, :] == blocks[:, None]
    listed = jnp.any(match, axis=1).astype(jnp.int32)
    slots = jnp.argmax(match, axis=1).astype(jnp.int32)
    source = slots // per
    place = ((source % 2) ^ core) * chips + ((source // 2) ^ chip)
    from_sibling = swap(siblings_part(got), "vocab", 1)
    seen = from_sibling[0, :TILE_ROWS, :BLK]
    seen = lax.optimization_barrier(seen) * jnp.bfloat16(0.5)
    placed = place_tiles(place * per + slots % per, listed, got, from_sibling, [seen])
    tiles = between_chips(placed)

    mass = jnp.sum(teacher, axis=1, dtype=jnp.float32)[None, :]

    logits, stats, kept, near, far = logits_and_stats(
        own, other, rows, weight, mass, width // data_size
    )
    own_cols = [swap_by_core(near), swap(far, "dp", data_size - 1)]

    stats = merge_pair(stats, swap(stats, "vocab", 1))
    all_stats = between_chips([stats] * chips)
    other_tiles = swap(siblings_part_after(tiles, rows, [stats]), "vocab", 1)
    spare = other_tiles[0, :TILE_ROWS, :BLK]
    grad_logits, share, rest, own_cols = logit_grads(
        logits, all_stats, tiles, other_tiles, weight, own_cols, [spare]
    )
    other_cols = swap(own_cols, "vocab", 1)

    share = share + swap(rest, "vocab", 1).astype(jnp.float32)
    shares = [share[j * rows : (j + 1) * rows] for j in range(chips)]
    count = 1
    while count < chips:
        for base in range(chips - 2 * count, -1, -2 * count):
            sent = swap(shares[base + count].astype(jnp.bfloat16), "vocab", 2 * count)
            shares[base] = shares[base] + sent.astype(jnp.float32)
        count *= 2
    grad_hidden = shares[0].astype(jnp.bfloat16)

    middle = grad_logits.shape[0] // 2
    near, far = swap(grad_logits, "dp", 1), swap(grad_logits, "dp", 2)
    last = [swap(near[:middle], "dp", 2), swap(far[middle:], "dp", 1)]
    partial = weight_grad_part([grad_logits, near, far], kept, own_cols, other_cols)
    grad_weight = weight_grad_rest(partial, last, own_cols, other_cols, [grad_hidden])
    return (grad_hidden, grad_weight)


def solution(mesh):
    placed = (P(("dp", "vocab"), None), P("vocab", None), P("dp", "vocab"), P("dp", None))

    def run(hidden, weight, teacher, block_ids):
        rows = hidden.shape[0] // (mesh.shape["dp"] * mesh.shape["vocab"])
        count = mesh.shape["vocab"]
        fits = count & (count - 1) == 0 and count > 2 and mesh.shape["dp"] == CORES**2
        fits = fits and rows % TILE_ROWS == 0 and BLK % rows == 0 and count * rows % (2 * BLK) == 0
        form = shards if fits else plain_shards
        return jax.shard_map(
            form,
            mesh=mesh,
            in_specs=placed,
            out_specs=(P(("dp", "vocab"), None), P("vocab", "dp")),
            check_vma=False,
        )(hidden, weight, teacher, block_ids)

    return run
```
